32 devices in a mesh: dp: 4 (over y, x), seq: 8 (over z, core).
Axes of the slice: x: 2, y: 2, z: 4, core: 2. Of those that a mesh axis runs over, the one named last changes fastest.
Arguments:
- block_input: bfloat16 [8192, 2048], P(('dp', 'seq')), may hold values from -6 to 6
- lengths: int32 [4, 2], P('dp'), may hold values from 1024 to 1024, as said below
- norm_gain: float32 [2048], replicated, may hold values from 0.25 to 1.75
- w_q: bfloat16 [2048, 2048], P('seq'), may hold values from -0.125 to 0.125
- w_f: bfloat16 [2048, 2048], P('seq'), may hold values from -0.125 to 0.125
- w_i: bfloat16 [2048, 2048], P('seq'), may hold values from -0.125 to 0.125
- w_g: bfloat16 [2048, 2048], P('seq'), may hold values from -0.125 to 0.125
- lower_bound: float32 [2048], replicated, may hold values from 0.7 to 1
- group_gain: float32 [128], replicated, may hold values from 0.25 to 1.75
- w_o: bfloat16 [2048, 2048], P('seq'), may hold values from -0.1875 to 0.1875
- ffn_norm_gain: float32 [2048], replicated, may hold values from 0.25 to 1.75
- w_gate: bfloat16 [2048, 5632], P('seq'), may hold values from -0.125 to 0.125
- w_up: bfloat16 [2048, 5632], P('seq'), may hold values from -0.125 to 0.125
- w_down: bfloat16 [5632, 2048], P('seq'), may hold values from -0.109375 to 0.109375
- out_grad: bfloat16 [8192, 2048], P(('dp', 'seq')), may hold values from -6 to 6
Outputs:
- out: bfloat16 [8192, 2048], P(('dp', 'seq'))
- input_grad: bfloat16 [8192, 2048], P(('dp', 'seq'))
- norm_gain_grad: float32 [2048], replicated
- w_q_grad: float32 [2048, 2048], P('seq')
- w_f_grad: float32 [2048, 2048], P('seq')
- w_i_grad: float32 [2048, 2048], P('seq')
- w_g_grad: float32 [2048, 2048], P('seq')
- lower_bound_grad: float32 [2048], replicated
- group_gain_grad: float32 [128], replicated
- w_o_grad: float32 [2048, 2048], P('seq')
- ffn_norm_gain_grad: float32 [2048], replicated
- w_gate_grad: float32 [2048, 5632], P('seq')
- w_up_grad: float32 [2048, 5632], P('seq')
- w_down_grad: float32 [5632, 2048], P('seq')
The draws below stay inside these ranges and needn't reach their ends.
Inputs may be any that keep to these rules, and one draw needn't show every extreme that they name: The lengths of each group sum to 2048.
All inputs are finite; a program needn't handle non-finite values.
Results may differ from the reference program's by a relative error of at most 0.02.
The reference program's roundings to bfloat16 on the way count: a program that leaves them out, or rounds other values in their place, can miss the bound.
Values may be sent and summed in bfloat16 or wider, within the bound.
No kernel may reach another device: no remote copies, remote signals or barrier semaphores. Data moves between devices by JAX's collectives and lax.ppermute only.
A program may use at most 512 MiB of HBM per device.

```python
import jax
import jax.numpy as jnp
from jax import lax

D = 2048
H = 16
DH = 128
FF = 5632
SPAN = 128
MIN_LEN = 1024
GROUPS = 4
SEQ_TOKENS = 2048
TOKENS = 8192


def draw_lengths(key, part):
    key = jax.random.fold_in(key, 11)
    first_key, order_key = jax.random.split(key)
    spare = SEQ_TOKENS - 2 * MIN_LEN
    drawn = MIN_LEN + jax.random.randint(first_key, (GROUPS,), 0, spare + 1)
    first = jnp.where(jnp.arange(GROUPS) == 0, MIN_LEN + spare, drawn)
    second = SEQ_TOKENS - first
    flip = jax.random.randint(order_key, (GROUPS,), 0, 2)
    leading = jnp.where(flip == 1, second, first)
    trailing = jnp.where(flip == 1, first, second)
    return jnp.stack([leading, trailing], axis=1).astype(jnp.int32)


def draw_lower_bound(key, part):
    key = jax.random.fold_in(key, 23)
    unit = jax.random.uniform(key, (D,), jnp.float32)
    lowest = jnp.log(0.5 / SEQ_TOKENS)
    top = jnp.log(0.3)
    return (1.0 - jnp.exp(lowest + (top - lowest) * unit)).astype(jnp.float32)


def shard_levels(own_key, dims, cuts, smallest, top_value):
    level, own = 1.0, jax.random.fold_in(own_key, 6)
    for dim, blocks in cuts:
        steps = jnp.exp(jax.random.uniform(jax.random.fold_in(own, dim), (blocks,), jnp.float32, smallest / len(cuts), top_value / len(cuts)))
        level = level * jnp.repeat(steps, dims[dim] // blocks).reshape([-1 if axis == dim else 1 for axis in range(len(dims))])
    return level


def centred(stream_key, dims, width, most, cuts=(), kind=jnp.bfloat16):
    level = shard_levels(stream_key, dims, cuts, -0.22, 0.18) if cuts else 1.0
    entries = jax.random.normal(stream_key, dims, jnp.float32) * width * level
    return jnp.minimum(jnp.maximum(entries, -most), most).astype(kind)


def setup_inputs(seed: int = 0) -> dict:
    key_list = jax.random.split(jax.random.key(seed), 16)
    return {
        "block_input": centred(key_list[0], (TOKENS, D), 1.0, 6.0, ((0, 32),)),
        "lengths": draw_lengths(jax.random.fold_in(key_list[15], 71), 0),
        "norm_gain": jnp.clip(1.0 + 0.15 * jax.random.normal(key_list[2], (D,), jnp.float32), 0.25, 1.75),
        "w_q": centred(key_list[3], (D, D), D ** -0.5, 0.125, ((0, 8),)),
        "w_f": centred(key_list[4], (D, D), D ** -0.5, 0.125, ((0, 8),)),
        "w_i": centred(key_list[5], (D, D), D ** -0.5, 0.125, ((0, 8),)),
        "w_g": centred(key_list[6], (D, D), D ** -0.5, 0.125, ((0, 8),)),
        "lower_bound": draw_lower_bound(jax.random.fold_in(key_list[15], 71), 0),
        "group_gain": jnp.clip(1.0 + 0.15 * jax.random.normal(key_list[8], (DH,), jnp.float32), 0.25, 1.75),
        "w_o": centred(key_list[9], (D, D), (D // 2) ** -0.5, 0.1875, ((0, 8),)),
        "ffn_norm_gain": jnp.clip(1.0 + 0.15 * jax.random.normal(key_list[10], (D,), jnp.float32), 0.25, 1.75),
        "w_gate": centred(key_list[11], (D, FF), D ** -0.5, 0.125, ((0, 8),)),
        "w_up": centred(key_list[12], (D, FF), D ** -0.5, 0.125, ((0, 8),)),
        "w_down": centred(key_list[13], (FF, D), (FF // 2) ** -0.5, 0.109375, ((0, 8),)),
        "out_grad": centred(key_list[14], (TOKENS, D), 1.0, 6.0, ((0, 32),)),
    }


@jax.custom_vjp
def low(v):
    return lax.optimization_barrier(v.astype(jnp.bfloat16)).astype(jnp.float32)

@jax.custom_vjp
def low_back(v):
    return v

def low_keep(v):
    return (low(v), None)

def low_pass(kept, grad):
    return (grad,)

def back_keep(v):
    return (v, None)

def back_low(kept, grad):
    return (low(grad),)
low.defvjp(low_keep, low_pass)
low_back.defvjp(back_keep, back_low)
EPS = 1e-06
HIGH = lax.Precision.HIGHEST

def matmul(left, right):
    return jnp.dot(left, right, precision=HIGH)

def silu(value):
    return value * jax.nn.sigmoid(value)

def rms_scale(value, gain):
    return value * lax.rsqrt(lax.optimization_barrier(jnp.mean(value * value, axis=-1, keepdims=True)) + EPS) * gain

def sequence_marks(lengths_row, positions):
    offsets = jnp.cumsum(lengths_row) - lengths_row
    seq_ids = lax.optimization_barrier(jnp.sum((positions[:, None] >= offsets[None, :]).astype(jnp.int32), axis=1)) - 1
    begins = lax.optimization_barrier(jnp.sum((positions[:, None] == offsets[None, :]).astype(jnp.float32), axis=1))
    return (seq_ids.astype(jnp.int32), begins)

def span_step(carry, block):
    state, decay = carry
    q_blk, k_blk, a_blk, v_blk, sid_blk, start_blk = block
    size = q_blk.shape[0]
    cumul = jnp.cumsum(a_blk, axis=0)
    inherit = (jnp.cumsum(start_blk) == 0).astype(jnp.float32)
    rows = lax.broadcasted_iota(jnp.int32, (size, size), 0)
    cols = lax.broadcasted_iota(jnp.int32, (size, size), 1)
    allowed = (sid_blk[:, None] == sid_blk[None, :]) & (cols <= rows)
    q_dec = q_blk * jnp.exp(cumul)
    k_dec = k_blk * jnp.exp(-cumul)
    scores = jnp.einsum('thi,shi->hts', q_dec, k_dec, precision=HIGH)
    scores = jnp.where(allowed[None], scores, 0.0)
    carried = jnp.einsum('thi,hij->thj', q_dec, state, precision=HIGH)
    out_blk = jnp.einsum('hts,shj->thj', scores, v_blk, precision=HIGH) + inherit[:, None, None] * carried
    from_start = q_dec * (decay[None] * inherit[:, None, None])
    last = cumul[-1]
    same_last = (sid_blk == sid_blk[-1]).astype(jnp.float32)
    tail = k_blk * jnp.exp(last[None] - cumul) * same_last[:, None, None]
    keep = inherit[-1]
    new_state = keep * jnp.exp(last)[:, :, None] * state + jnp.einsum('shi,shj->hij', tail, v_blk, precision=HIGH)
    new_decay = decay * jnp.exp(last) * keep
    return ((new_state, new_decay), (out_blk, from_start))

def group_forward(group_rows, lengths_row, norm_gain, w_q, w_f, w_i, w_g, lower_bound, group_gain, w_o, ffn_norm_gain, w_gate, w_up, w_down):
    count = group_rows.shape[0]
    seq_ids, begins = sequence_marks(lengths_row, jnp.arange(count, dtype=jnp.int32))
    hnorm = low(rms_scale(group_rows, norm_gain))
    qz = low_back(matmul(hnorm, w_q))
    fz = low_back(matmul(hnorm, w_f))
    vz = low_back(matmul(hnorm, w_i))
    gz = low_back(matmul(hnorm, w_g))
    query = silu(qz)
    forget = lower_bound + (1.0 - lower_bound) * jax.nn.sigmoid(fz)
    keyed = 1.0 - forget
    log_forget = jnp.log(forget)

    def split(value):
        return value.reshape(count // SPAN, SPAN, H, DH)
    blocks = (split(query), split(keyed), split(log_forget), split(vz), seq_ids.reshape(-1, SPAN), begins.reshape(-1, SPAN))
    start_carry = (jnp.zeros((H, DH, DH), jnp.float32), jnp.ones((H, DH), jnp.float32))
    unused, (outs, skipped) = lax.scan(jax.checkpoint(span_step), start_carry, blocks)
    mixed = outs.reshape(count, H, DH)
    normed = mixed * lax.rsqrt(lax.optimization_barrier(jnp.mean(mixed * mixed, axis=-1, keepdims=True)) + EPS) * group_gain
    gated = low(normed.reshape(count, D) * silu(gz))
    resid = group_rows + low_back(matmul(gated, w_o))
    hnorm_two = low(rms_scale(resid, ffn_norm_gain))
    gate = low_back(matmul(hnorm_two, w_gate))
    upper = low_back(matmul(hnorm_two, w_up))
    hidden = low(silu(gate) * upper)
    return resid + matmul(hidden, w_down)

def reference(block_input, lengths, norm_gain, w_q, w_f, w_i, w_g, lower_bound, group_gain, w_o, ffn_norm_gain, w_gate, w_up, w_down, out_grad):

    def forward(all_input, norm_gain, w_q, w_f, w_i, w_g, lower_bound, group_gain, w_o, ffn_norm_gain, w_gate, w_up, w_down):

        def one_group(pair):
            return group_forward(pair[0], pair[1], norm_gain, w_q, w_f, w_i, w_g, lower_bound, group_gain, w_o, ffn_norm_gain, w_gate, w_up, w_down)
        groups_out = lax.map(jax.checkpoint(one_group), (all_input.reshape(GROUPS, SEQ_TOKENS, D), lengths))
        return groups_out.reshape(TOKENS, D)
    params = (block_input.astype(jnp.float32), norm_gain, w_q.astype(jnp.float32), w_f.astype(jnp.float32), w_i.astype(jnp.float32), w_g.astype(jnp.float32), lower_bound, group_gain, w_o.astype(jnp.float32), ffn_norm_gain, w_gate.astype(jnp.float32), w_up.astype(jnp.float32), w_down.astype(jnp.float32))
    result, pull = jax.vjp(forward, *params)
    grads = pull(out_grad.astype(jnp.float32))
    return (result.astype(jnp.bfloat16), grads[0].astype(jnp.bfloat16), grads[1], grads[2], grads[3], grads[4], grads[5], grads[6], grads[7], grads[8], grads[9], grads[10], grads[11], grads[12])
```

```python
import functools

import jax
import jax.numpy as jnp
from jax import lax
from jax.experimental import pallas as pl
from jax.experimental.pallas import tpu as pltpu
from jax.sharding import PartitionSpec as P

EPS = 1e-06
MIN_LEN = 1024
BF = jnp.bfloat16
F32 = jnp.float32


def sigmoid(value):
    return jax.nn.sigmoid(value)


def silu(value):
    return value * sigmoid(value)


def silu_grad(value):
    s = sigmoid(value)
    return s * (1.0 + value * (1.0 - s))


def mm(left, right, kind=F32):
    return jnp.dot(left, right, preferred_element_type=F32).astype(kind)


def dot_first(left, right, kind=F32):
    return lax.dot_general(
        left, right, (((0,), (0,)), ((), ())), preferred_element_type=F32
    ).astype(kind)


def dot_last(left, right, kind=F32):
    return lax.dot_general(
        left, right, (((1,), (1,)), ((), ())), preferred_element_type=F32
    ).astype(kind)


def swap(value, bits):
    count = lax.axis_size("dp")
    return lax.ppermute(value, "dp", [(s, s ^ bits) for s in range(count)])


def gather_dp(own):
    half = own.shape[0] // 2
    one, two = swap(own, 1), swap(own, 2)
    top, bottom = swap(one[:half], 2), swap(two[half:], 1)
    return jnp.concatenate([own, one, two, top, bottom], axis=0)


def scatter_dp(parts):
    rows = parts.shape[0] // 4
    half = rows // 2
    p0, p1, p2, p3 = (parts[k * rows : (k + 1) * rows] for k in range(4))
    top, bottom = swap(p3[:half], 1), swap(p3[half:], 2)
    one_a, two_b = swap(p1[:half], 1), swap(p2[half:], 2)
    two_a = swap((p2[:half].astype(F32) + top.astype(F32)).astype(BF), 2)
    one_b = swap((p1[half:].astype(F32) + bottom.astype(F32)).astype(BF), 1)
    one = jnp.concatenate([one_a, one_b], axis=0).astype(F32)
    two = jnp.concatenate([two_a, two_b], axis=0).astype(F32)
    return p0.astype(F32) + one + two


def absolute(blocks):
    place = lax.axis_index("dp")
    odd, high = (place & 1) == 1, (place & 2) == 2
    a, b, c, d = blocks
    a, b = jnp.where(odd, b, a), jnp.where(odd, a, b)
    c, d = jnp.where(odd, d, c), jnp.where(odd, c, d)
    return (
        jnp.where(high, c, a),
        jnp.where(high, d, b),
        jnp.where(high, a, c),
        jnp.where(high, b, d),
    )


def marks(starts_ref, slot, size, count):
    col = lax.broadcasted_iota(jnp.int32, (size, 1), 0)
    row = lax.broadcasted_iota(jnp.int32, (1, size), 1)
    sid_c = jnp.zeros((size, 1), jnp.int32)
    sid_r = jnp.zeros((1, size), jnp.int32)
    sid_last = jnp.int32(0)
    begun = jnp.zeros((size, 1), jnp.int32)
    ended = jnp.int32(0)
    for j in range(count):
        at = starts_ref[slot, j]
        sid_c += (col >= at).astype(jnp.int32)
        sid_r += (row >= at).astype(jnp.int32)
        sid_last += (size - 1 >= at).astype(jnp.int32)
        begun += ((col >= at) & (at >= 0)).astype(jnp.int32)
        ended += ((size - 1 >= at) & (at >= 0)).astype(jnp.int32)
    inherit = (begun == 0).astype(F32)
    same_last = (sid_c == sid_last).astype(F32)
    keep = (ended == 0).astype(F32)
    return sid_c, sid_r, inherit, same_last, keep


def split_dot(left, value):
    high = value.astype(BF)
    low = (value - high.astype(F32)).astype(BF)
    return mm(left, high) + mm(left, low)


def gates(f, bound):
    sg = sigmoid(f)
    forget = bound + (1.0 - bound) * sg
    return sg, forget, (1.0 - bound) * (1.0 - sg), jnp.log(forget)


def about_middle(size):
    rows = lax.broadcasted_iota(jnp.int32, (size, size), 0)
    cols = lax.broadcasted_iota(jnp.int32, (size, size), 1)
    return (cols <= rows).astype(BF) - (cols < size // 2).astype(BF)


def end_kernel(count, starts, f_ref, v_ref, b_ref, pack_ref):
    size = f_ref.shape[0]
    slot = pl.program_id(1)
    _, _, _, same_last, keep = marks(starts, slot, size, count)
    _, _, k, a = gates(f_ref[...], b_ref[...])
    cm = split_dot(about_middle(size), a)
    last = cm[size - 1 :]
    total = jnp.sum(a, axis=0, keepdims=True)
    tail = (k * jnp.exp(last - cm) * same_last).astype(BF)
    pack_ref[0, :128] = dot_first(v_ref[...].astype(BF), tail).astype(BF)
    pack_ref[0, 128:] = jnp.broadcast_to(jnp.exp(total) * keep, (16, 128)).astype(BF)


def intra_kernel(count, starts, q_ref, f_ref, v_ref, b_ref, out_ref, qs_ref):
    size = f_ref.shape[0]
    slot = pl.program_id(1)
    sid_c, sid_r, inherit, _, _ = marks(starts, slot, size, count)
    _, _, k, a = gates(f_ref[...], b_ref[...])
    cm = split_dot(about_middle(size), a)
    mid = jnp.sum(a[: size // 2], axis=0, keepdims=True)
    q = silu(q_ref[...])
    qd = q * jnp.exp(cm)
    kd = k * jnp.exp(-cm)
    rows = lax.broadcasted_iota(jnp.int32, (size, size), 0)
    cols = lax.broadcasted_iota(jnp.int32, (size, size), 1)
    scores = jnp.where((cols <= rows) & (sid_c == sid_r), dot_last(qd.astype(BF), kd.astype(BF)), 0.0)
    out_ref[...] = mm(scores.astype(BF), v_ref[...].astype(BF))
    qs_ref[...] = (q * jnp.exp(cm + mid) * inherit).astype(BF)


def chained(packs):
    total = packs[-1][0, :128].astype(F32)
    for p in packs[-2::-1]:
        total = p[0, :128].astype(F32) + p[0, 128:].astype(F32)[:1] * total
    return total


def mixed_kernel(hops, out_ref, qs_ref, g_ref, gain_ref, *rest):
    packs, (mixed_ref, on_ref, enter_ref) = rest[:hops], rest[hops:]
    enter = chained(packs)
    enter_ref[0] = enter
    mixed = out_ref[...] + dot_last(qs_ref[...], enter.astype(BF))
    mixed_ref[...] = mixed
    r = lax.rsqrt(jnp.mean(mixed * mixed, axis=-1, keepdims=True) + EPS)
    on_ref[...] = (mixed * r * gain_ref[...] * silu(g_ref[...])).astype(BF)


def norm_back_kernel(
    don_ref, g_ref, mixed_ref, qs_ref, gain_ref, pack_ref, dmix_ref, dg_ref, dpack_ref, dgain_ref
):
    don, gz, mixed, gain = don_ref[...], g_ref[...], mixed_ref[...], gain_ref[...]
    sg = sigmoid(gz)
    s = gz * sg
    r = lax.rsqrt(jnp.mean(mixed * mixed, axis=-1, keepdims=True) + EPS)
    n = mixed * r
    w = don * gain * s
    dmix = (r * (w - n * jnp.mean(w * n, axis=-1, keepdims=True))).astype(BF)
    dmix_ref[...] = dmix
    dg_ref[...] = (don * gain * n * (sg * (1.0 + gz * (1.0 - sg)))).astype(BF)
    dpack_ref[0, :128] = dot_first(dmix, qs_ref[...]).astype(BF)
    dpack_ref[0, 128:] = pack_ref[0, 128:]

    @pl.when((pl.program_id(0) == 0) & (pl.program_id(1) == 0))
    def _():
        dgain_ref[...] = jnp.zeros_like(dgain_ref)

    dgain_ref[...] += jnp.sum(don * s * n, axis=0, keepdims=True)


def back_kernel(count, hops, starts, q_ref, f_ref, v_ref, b_ref, dmix_ref, enter_ref, *rest):
    packs, (dq_ref, df_ref, dv_ref, db_ref) = rest[:hops], rest[hops:]
    size = f_ref.shape[0]
    slot = pl.program_id(1)
    sid_c, sid_r, inherit, same_last, keep = marks(starts, slot, size, count)
    bound = b_ref[...]
    sg, forget, k, a = gates(f_ref[...], bound)
    cm = split_dot(about_middle(size), a)
    last = cm[size - 1 :]
    mid = jnp.sum(a[: size // 2], axis=0, keepdims=True)
    qz = q_ref[...]
    sq = sigmoid(qz)
    up, down = jnp.exp(cm), jnp.exp(-cm)
    qd = (qz * sq * up).astype(BF)
    kd = (k * down).astype(BF)
    v = v_ref[...].astype(BF)
    dmix = dmix_ref[...]
    rows = lax.broadcasted_iota(jnp.int32, (size, size), 0)
    cols = lax.broadcasted_iota(jnp.int32, (size, size), 1)
    same = sid_c == sid_r
    allowed = (cols <= rows) & same
    scores = jnp.where(allowed, dot_last(qd, kd), 0.0).astype(BF)
    dscores = jnp.where(allowed, dot_last(dmix, v), 0.0).astype(BF)
    enter = enter_ref[0]
    leave = chained(packs)
    leave_low = (leave * jnp.exp(last)).astype(BF)
    enter_low = (enter * jnp.exp(mid)).astype(BF)
    dqd = mm(dscores, kd) + inherit * mm(dmix, enter_low)
    dkd_tail = same_last * mm(v, leave_low)
    dkd = dot_first(dscores, qd) + dkd_tail
    dv = dot_first(scores, dmix) + same_last * dot_last(kd, leave_low)
    qd, kd = qd.astype(F32), kd.astype(F32)
    dlog = dqd * qd - dkd * kd
    whole = jnp.sum(dkd_tail * kd, axis=0, keepdims=True) + keep * jnp.exp(mid + last) * jnp.sum(
        leave * enter, axis=0, keepdims=True
    )
    after = ((cols >= rows) & same).astype(BF)
    da = split_dot(after, dlog) + same_last * whole
    dforget = da / forget - dkd * down
    dq_ref[...] = (dqd * up * (sq * (1.0 + qz * (1.0 - sq)))).astype(BF)
    df_ref[...] = (dforget * (1.0 - bound) * sg * (1.0 - sg)).astype(BF)
    dv_ref[...] = dv.astype(BF)

    @pl.when(slot == 0)
    def _():
        db_ref[...] = jnp.zeros_like(db_ref)

    db_ref[0] += jnp.sum(dforget * (1.0 - sg), axis=0, keepdims=True)


def tile(size, base):
    return pl.BlockSpec((size, 128), lambda h, s, *_: (s, h + base))


def state(rows, heads):
    return pl.BlockSpec((1, rows, 128), lambda h, s, *_: (s * heads + h, 0, 0))


def per_head():
    return pl.BlockSpec((1, 128), lambda h, s, *_: (0, h))


def fixed():
    return pl.BlockSpec((1, 128), lambda h, s, *_: (0, 0))


def call(kernel, grid, scalars, in_specs, out_specs, out_shape, args):
    params = pltpu.CompilerParams(vmem_limit_bytes=48 * 1024 * 1024)
    return pl.pallas_call(
        kernel,
        grid_spec=pltpu.PrefetchScalarGridSpec(
            num_scalar_prefetch=len(scalars), grid=grid, in_specs=in_specs, out_specs=out_specs
        ),
        out_shape=out_shape,
        compiler_params=params,
    )(*scalars, *args)


def reached(pack, forward, tokens):
    count = lax.axis_size("seq")
    if count * tokens == 2 * MIN_LEN and MIN_LEN % tokens == 0:
        span = MIN_LEN // tokens
        out = []
        for hop in range(1, span):
            pairs = [(s, s + hop) for s in range(count) if s // span == (s + hop) // span]
            if not forward:
                pairs = [(b, a) for a, b in pairs]
            out.append(lax.ppermute(pack, "seq", pairs))
        return out
    place = lax.axis_index("seq")
    every = lax.all_gather(pack, "seq")
    shape = (pack.shape[0], 128, pack.shape[2])

    def one(k, total):
        at = k if forward else count - 1 - k
        there = lax.dynamic_index_in_dim(every, at, 0, False).astype(F32)
        new = there[:, :128] + there[:, 128:129] * total
        return jnp.where((at < place) if forward else (at > place), new, total)

    total = lax.fori_loop(0, count, one, jnp.zeros(shape, F32))
    return [jnp.concatenate([total, jnp.zeros_like(total[:, :16])], axis=1).astype(BF)]


def shards(
    block_input,
    lengths,
    norm_gain,
    w_q,
    w_f,
    w_i,
    w_g,
    lower_bound,
    group_gain,
    w_o,
    ffn_norm_gain,
    w_gate,
    w_up,
    w_down,
    out_grad,
):
    tokens, width = block_input.shape
    head_dim = group_gain.shape[0]
    heads = width // head_dim // 4
    mine = heads * head_dim
    seqs = lax.axis_size("seq")
    dp = lax.axis_index("dp")
    low_bit, high_bit = dp & 1, dp >> 1

    def of_heads(value, axis):
        shape = value.shape
        cut = value.reshape(shape[:axis] + (2, heads, 2, head_dim) + shape[axis + 1 :])
        cut = lax.dynamic_index_in_dim(cut, high_bit, axis + 2, False)
        cut = lax.dynamic_index_in_dim(cut, low_bit, axis, False)
        return cut.reshape(shape[:axis] + (mine,) + shape[axis + 1 :])

    def to_heads(blocks, axis):
        a, b, c, d = absolute(blocks)
        shape = a.shape
        cut = [v.reshape(shape[:axis] + (heads, head_dim) + shape[axis + 1 :]) for v in (a, b, c, d)]
        pair = [jnp.stack([cut[k], cut[k + 2]], axis=axis + 1) for k in range(2)]
        full = jnp.stack(pair, axis=axis)
        return full.reshape(shape[:axis] + (4 * mine,) + shape[axis + 1 :])

    chunk = w_down.shape[0] // 4
    ff = chunk * seqs

    def of_hidden(value):
        cut = value.reshape(value.shape[0], seqs, 4, chunk)
        return lax.dynamic_index_in_dim(cut, dp, 2, False).reshape(value.shape[0], ff)

    def to_hidden(blocks):
        cut = [v.reshape(v.shape[0], seqs, 1, chunk) for v in absolute(blocks)]
        return jnp.concatenate(cut, axis=2).reshape(blocks[0].shape[0], 4 * ff)

    def gather_seq(value):
        return lax.all_gather(value, "seq", axis=0, tiled=True)

    def scatter_seq(value):
        return lax.psum_scatter(value.astype(BF), "seq", scatter_dimension=0, tiled=True)

    def blocks_dp(value):
        rows = value.shape[0]
        full = gather_dp(value)
        return [full[k * rows : (k + 1) * rows] for k in range(4)]

    wfv = gather_seq(jnp.concatenate([of_heads(w_f, 1), of_heads(w_i, 1)], axis=1))
    wqg = gather_seq(jnp.concatenate([of_heads(w_q, 1), of_heads(w_g, 1)], axis=1))
    natural = w_o.shape[0] == 2 * head_dim
    if natural:
        part = lax.dynamic_slice_in_dim(w_o, high_bit * head_dim, head_dim, 0)
        wo = lax.dynamic_slice_in_dim(gather_seq(part), low_bit * mine, mine, 0)
    else:
        wo = of_heads(gather_seq(w_o), 0)
    wgu = gather_seq(jnp.concatenate([of_hidden(w_gate), of_hidden(w_up)], axis=1))
    wd = gather_seq(lax.dynamic_slice_in_dim(w_down, dp * chunk, chunk, 0))

    x = block_input.astype(F32)
    r1 = lax.rsqrt(jnp.mean(x * x, axis=-1, keepdims=True) + EPS)
    h = (x * r1 * norm_gain).astype(BF)
    h_all = gather_dp(h)

    starts = jnp.cumsum(lengths[0]) - lengths[0] - lax.axis_index("seq") * tokens
    starts = jnp.stack([starts] + [swap(starts, k) for k in (1, 2, 3)])
    count = lengths.shape[1]
    bound = of_heads(lower_bound, 0)[None]
    gain = group_gain[None]

    zfv = mm(h_all, wfv)
    zqg = mm(h_all, wqg)
    og_all = gather_dp(out_grad)

    grid = (heads, 4)
    pairs = heads * 4
    rows = 4 * tokens
    wide = jax.ShapeDtypeStruct((rows, mine), F32)
    thin = jax.ShapeDtypeStruct((rows, mine), BF)
    packed = jax.ShapeDtypeStruct((pairs, 144, 128), BF)
    ql, fl, vl, gl = tile(tokens, 0), tile(tokens, 0), tile(tokens, heads), tile(tokens, heads)
    plain = tile(tokens, 0)
    pack_spec, state_spec = state(144, heads), state(128, heads)

    pack = call(
        functools.partial(end_kernel, count), grid, (starts,),
        [fl, vl, per_head()], pack_spec, packed, (zfv, zfv, bound),
    )
    before = reached(pack, True, tokens)
    intra, qs = call(
        functools.partial(intra_kernel, count), grid, (starts,),
        [ql, fl, vl, per_head()], [plain, plain], [wide, thin], (zqg, zfv, zfv, bound),
    )
    mixed, on, enter = call(
        functools.partial(mixed_kernel, len(before)), grid, (),
        [plain, plain, gl, fixed()] + [pack_spec] * len(before),
        [plain, plain, state_spec],
        [wide, thin, jax.ShapeDtypeStruct((pairs, 128, 128), F32)],
        (intra, qs, zqg, gain, *before),
    )

    y = x + scatter_dp(mm(on, wo, BF))
    r2 = lax.rsqrt(jnp.mean(y * y, axis=-1, keepdims=True) + EPS)
    h2_all = gather_dp((y * r2 * ffn_norm_gain).astype(BF))

    gu = mm(h2_all, wgu)
    gate, upper = gu[:, :ff], gu[:, ff:]
    hidden = (silu(gate) * upper).astype(BF)
    d_hidden = dot_last(og_all, wd)
    d_gate = (d_hidden * upper * silu_grad(gate)).astype(BF)
    d_upper = (d_hidden * silu(gate)).astype(BF)
    d_gu = jnp.concatenate([d_gate, d_upper], axis=1)
    d_h2 = scatter_dp(dot_last(d_gu, wgu, BF))
    result = (y + scatter_dp(mm(hidden, wd, BF))).astype(BF)

    down_rows = scatter_seq(dot_first(hidden, og_all, BF))
    gate_rows = scatter_seq(dot_first(h2_all, d_gate, BF))
    up_rows = scatter_seq(dot_first(h2_all, d_upper, BF))

    og = out_grad.astype(F32)
    d_ffn_gain = jnp.sum(d_h2 * y * r2, axis=0)
    u2 = d_h2 * ffn_norm_gain
    d_y = og + r2 * u2 - y * (r2 * r2 * r2) * jnp.mean(u2 * y, axis=-1, keepdims=True)
    d_branch = gather_dp(d_y.astype(BF))

    d_on = dot_last(d_branch, wo)
    d_mixed, d_gz, d_pack, d_gain = call(
        norm_back_kernel, grid, (),
        [plain, gl, plain, plain, fixed(), pack_spec],
        [plain, plain, pack_spec, fixed()],
        [thin, thin, packed, jax.ShapeDtypeStruct((1, 128), F32)],
        (d_on, zqg, mixed, qs, gain, pack),
    )
    after = reached(d_pack, False, tokens)
    d_qz, d_fz, d_vz, d_bound = call(
        functools.partial(back_kernel, count, len(after)), grid, (starts,),
        [ql, fl, vl, per_head(), plain, state_spec] + [pack_spec] * len(after),
        [plain, plain, plain, pl.BlockSpec((1, 1, 128), lambda h, s, *_: (h, 0, 0))],
        [thin, thin, thin, jax.ShapeDtypeStruct((heads, 1, 128), F32)],
        (zqg, zfv, zfv, bound, d_mixed, enter, *after),
    )

    d_fv = jnp.concatenate([d_fz, d_vz], axis=1)
    d_qg = jnp.concatenate([d_qz, d_gz], axis=1)
    d_h = scatter_dp((dot_last(d_fv, wfv) + dot_last(d_qg, wqg)).astype(BF))

    o_part = dot_first(on, d_branch, BF)
    if natural:
        none = jnp.zeros_like(o_part)
        o_full = jnp.where(
            low_bit == 0,
            jnp.concatenate([o_part, none], axis=0),
            jnp.concatenate([none, o_part], axis=0),
        )
        o_rows = scatter_seq(o_full)
        o_mine = o_rows + swap(o_rows, 1)
        o_other = swap(o_mine, 2)
        grad_o = jnp.where(
            high_bit == 0,
            jnp.concatenate([o_mine, o_other], axis=0),
            jnp.concatenate([o_other, o_mine], axis=0),
        ).astype(F32)
    else:
        none = jnp.zeros_like(o_part)
        o_full = to_heads([o_part, none, none, none], 0)
        grad_o = lax.psum(scatter_seq(o_full).astype(F32), "dp")

    grad_down = jnp.concatenate(absolute(blocks_dp(down_rows)), axis=0).astype(F32)
    grad_gate = to_hidden(blocks_dp(gate_rows)).astype(F32)
    grad_up = to_hidden(blocks_dp(up_rows)).astype(F32)

    def head_grad(value):
        return to_heads(blocks_dp(scatter_seq(dot_first(h_all, value, BF))), 1).astype(F32)

    grad_g = head_grad(d_gz)
    grad_f = head_grad(d_fz)
    grad_i = head_grad(d_vz)
    grad_q = head_grad(d_qz)

    d_norm_gain = jnp.sum(d_h * x * r1, axis=0)
    u1 = d_h * norm_gain
    d_x = d_y + r1 * u1 - x * (r1 * r1 * r1) * jnp.mean(u1 * x, axis=-1, keepdims=True)

    zero = jnp.zeros((mine,), F32)
    d_bound = to_heads([d_bound.reshape(mine), zero, zero, zero], 0)
    small = lax.psum((d_norm_gain, d_ffn_gain, d_gain[0], d_bound), ("dp", "seq"))
    return (
        result,
        d_x.astype(BF),
        small[0],
        grad_q,
        grad_f,
        grad_i,
        grad_g,
        small[3],
        small[2],
        grad_o,
        small[1],
        grad_gate,
        grad_up,
        grad_down,
    )


def solution(mesh):
    both = P(("dp", "seq"), None)
    rows = P("seq", None)
    return jax.shard_map(
        shards,
        mesh=mesh,
        in_specs=(
            both, P("dp", None), P(), rows, rows, rows, rows, P(), P(), rows, P(), rows, rows, rows, both,
        ),
        out_specs=(
            both, both, P(), rows, rows, rows, rows, P(), P(), rows, P(), rows, rows, rows,
        ),
        check_vma=False,
    )
```

```python
import functools

import jax
import jax.numpy as jnp
from jax import lax
from jax.experimental import pallas as pl
from jax.experimental.pallas import tpu as pltpu
from jax.sharding import PartitionSpec as P

EPS = 1e-06
MIN_LEN = 1024
BF = jnp.bfloat16
F32 = jnp.float32


def sigmoid(value):
    return jax.nn.sigmoid(value)


def silu(value):
    return value * sigmoid(value)


def silu_grad(value):
    s = sigmoid(value)
    return s * (1.0 + value * (1.0 - s))


def mm(left, right, kind=F32):
    return jnp.dot(left, right, preferred_element_type=F32).astype(kind)


def dot_first(left, right, kind=F32):
    return lax.dot_general(
        left, right, (((0,), (0,)), ((), ())), preferred_element_type=F32
    ).astype(kind)


def dot_last(left, right, kind=F32):
    return lax.dot_general(
        left, right, (((1,), (1,)), ((), ())), preferred_element_type=F32
    ).astype(kind)


def swap(value, bits):
    count = lax.axis_size("dp")
    return lax.ppermute(value, "dp", [(s, s ^ bits) for s in range(count)])


def gather_parts(own):
    half = own.shape[0] // 2
    one, two = swap(own, 1), swap(own, 2)
    top, bottom = swap(one[:half], 2), swap(two[half:], 1)
    return own, one, two, top, bottom


def gather_dp(own):
    return jnp.concatenate(gather_parts(own), axis=0)


def scatter_begin(parts):
    rows = parts.shape[0] // 4
    half = rows // 2
    p0, p1, p2, p3 = (parts[k * rows : (k + 1) * rows] for k in range(4))
    top, bottom = swap(p3[:half], 1), swap(p3[half:], 2)
    one_a, two_b = swap(p1[:half], 1), swap(p2[half:], 2)
    two_a = (p2[:half].astype(F32) + top.astype(F32)).astype(BF)
    one_b = (p1[half:].astype(F32) + bottom.astype(F32)).astype(BF)
    return (two_a, one_b), (p0, one_a, two_b)


def scatter_end(onward, at_hand):
    p0, one_a, two_b = at_hand
    two_a, one_b = swap(onward[0], 2), swap(onward[1], 1)
    one = jnp.concatenate([one_a, one_b], axis=0).astype(F32)
    two = jnp.concatenate([two_a, two_b], axis=0).astype(F32)
    return p0.astype(F32) + one + two


def scatter_dp(parts):
    return scatter_end(*scatter_begin(parts))


def later(value, *needed):
    return lax.optimization_barrier((value, needed))[0]


def pair_halves(own, other, place, heads):
    width = own.shape[1]
    own, other = (v.reshape(heads, 1, -1, width) for v in (own, other))
    both = jnp.where(
        place == 0,
        jnp.concatenate([own, other], axis=1),
        jnp.concatenate([other, own], axis=1),
    )
    return both.reshape(-1, width)


def absolute(blocks):
    place = lax.axis_index("dp")
    odd, high = (place & 1) == 1, (place & 2) == 2
    a, b, c, d = blocks
    a, b = jnp.where(odd, b, a), jnp.where(odd, a, b)
    c, d = jnp.where(odd, d, c), jnp.where(odd, c, d)
    return (
        jnp.where(high, c, a),
        jnp.where(high, d, b),
        jnp.where(high, a, c),
        jnp.where(high, b, d),
    )


def marks(starts_ref, size, count):
    slot = pl.program_id(0)
    col = lax.broadcasted_iota(jnp.int32, (size, 1), 0)
    row = lax.broadcasted_iota(jnp.int32, (1, size), 1)
    sid_c = jnp.zeros((size, 1), jnp.int32)
    sid_r = jnp.zeros((1, size), jnp.int32)
    sid_last = jnp.int32(0)
    begun = jnp.zeros((size, 1), jnp.int32)
    ended = jnp.int32(0)
    for j in range(count):
        at = starts_ref[slot, j]
        sid_c += (col >= at).astype(jnp.int32)
        sid_r += (row >= at).astype(jnp.int32)
        sid_last += (size - 1 >= at).astype(jnp.int32)
        begun += ((col >= at) & (at >= 0)).astype(jnp.int32)
        ended += ((size - 1 >= at) & (at >= 0)).astype(jnp.int32)
    inherit = (begun == 0).astype(F32)
    same_last = (sid_c == sid_last).astype(F32)
    keep = (ended == 0).astype(F32)
    return sid_c == sid_r, inherit, same_last, keep


def split_dot(left, value):
    high = value.astype(BF)
    low = (value - high.astype(F32)).astype(BF)
    return mm(left, high) + mm(left, low)


def halves_of(value):
    high = value.astype(BF)
    return high, (value - high.astype(F32)).astype(BF)


def scores_of(qd, kd):
    (qh, ql), (kh, kl) = halves_of(qd), halves_of(kd)
    return dot_last(qh, kh) + (dot_last(qh, kl) + dot_last(ql, kh)), qh, kh


def gates(f, bound):
    sg = sigmoid(f)
    forget = bound + (1.0 - bound) * sg
    return sg, forget, (1.0 - bound) * (1.0 - sg), jnp.log(forget)


def positions(size):
    rows = lax.broadcasted_iota(jnp.int32, (size, size), 0)
    cols = lax.broadcasted_iota(jnp.int32, (size, size), 1)
    return rows, cols


def about_middle(size):
    rows, cols = positions(size)
    return (cols <= rows).astype(BF) - (cols < size // 2).astype(BF)


def each(heads):
    return [(k, slice(128 * k, 128 * (k + 1))) for k in range(heads)]


def end_kernel(count, heads, starts, f_ref, v_ref, b_ref, pack_ref):
    size = f_ref.shape[0]
    _, _, same_last, keep = marks(starts, size, count)
    middle = about_middle(size)
    for k, at in each(heads):
        _, _, key, a = gates(f_ref[:, at], b_ref[:, at])
        cm = split_dot(middle, a)
        total = jnp.sum(a, axis=0, keepdims=True)
        tail = (key * jnp.exp(cm[size - 1 :] - cm) * same_last).astype(BF)
        pack_ref[k, :128] = dot_first(v_ref[:, at].astype(BF), tail).astype(BF)
        pack_ref[k, 128:] = jnp.broadcast_to(jnp.exp(total) * keep, (16, 128)).astype(BF)


def intra_kernel(count, heads, starts, f_ref, v_ref, q_ref, b_ref, out_ref, qs_ref):
    size = f_ref.shape[0]
    same, inherit, _, _ = marks(starts, size, count)
    middle = about_middle(size)
    rows, cols = positions(size)
    allowed = (cols <= rows) & same
    for _, at in each(heads):
        _, _, key, a = gates(f_ref[:, at], b_ref[:, at])
        cm = split_dot(middle, a)
        mid = jnp.sum(a[: size // 2], axis=0, keepdims=True)
        q = silu(q_ref[:, at])
        scores = jnp.where(allowed, scores_of(q * jnp.exp(cm), key * jnp.exp(-cm))[0], 0.0)
        out_ref[:, at] = mm(scores.astype(BF), v_ref[:, at].astype(BF))
        qs_ref[:, at] = (q * jnp.exp(cm + mid) * inherit).astype(BF)


def join_kernel(near_ref, far_ref, out_ref):
    near, far = near_ref[...].astype(F32), far_ref[...].astype(F32)
    decay = near[:, 128:129]
    out_ref[:, :128] = (near[:, :128] + decay * far[:, :128]).astype(BF)
    out_ref[:, 128:] = (near[:, 128:] * far[:, 128:]).astype(BF)


def reach(near_ref, far_ref, whole_ref, k):
    decay = jnp.where(whole_ref[0] == 1, near_ref[k, 128:].astype(F32)[:1], 1.0)
    return near_ref[k, :128].astype(F32) + decay * far_ref[k, :128].astype(F32)


def mixed_kernel(
    heads, whole, out_ref, qs_ref, g_ref, gain_ref, near_ref, far_ref, mixed_ref, on_ref, enter_ref
):
    for k, at in each(heads):
        enter = reach(near_ref, far_ref, whole, k)
        enter_ref[k] = enter
        mixed = out_ref[:, at] + dot_last(qs_ref[:, at], enter.astype(BF))
        mixed_ref[:, at] = mixed
        r = lax.rsqrt(jnp.mean(mixed * mixed, axis=-1, keepdims=True) + EPS)
        on_ref[:, at] = (mixed * r * gain_ref[...] * silu(g_ref[:, at])).astype(BF)


def norm_back_kernel(
    heads, don_ref, g_ref, mixed_ref, qs_ref, gain_ref, pack_ref, dmix_ref, dg_ref, dpack_ref, dgain_ref
):
    @pl.when(pl.program_id(0) == 0)
    def _():
        dgain_ref[...] = jnp.zeros_like(dgain_ref)

    gain = gain_ref[...]
    for k, at in each(heads):
        don, gz, mixed = don_ref[:, at], g_ref[:, at], mixed_ref[:, at]
        sg = sigmoid(gz)
        s = gz * sg
        r = lax.rsqrt(jnp.mean(mixed * mixed, axis=-1, keepdims=True) + EPS)
        n = mixed * r
        w = don * gain * s
        dmix = r * (w - n * jnp.mean(w * n, axis=-1, keepdims=True))
        dmix_ref[:, at] = dmix
        dg_ref[:, at] = (don * gain * n * (sg * (1.0 + gz * (1.0 - sg)))).astype(BF)
        dpack_ref[k, :128] = dot_first(dmix.astype(BF), qs_ref[:, at]).astype(BF)
        dpack_ref[k, 128:] = pack_ref[k, 128:]
        dgain_ref[...] += jnp.sum(don * s * n, axis=0, keepdims=True)


def back_kernel(
    count, heads, starts, whole, f_ref, v_ref, q_ref, b_ref, dg_ref, dmix_ref, enter_ref, near_ref,
    far_ref, dz_ref, db_ref,
):
    @pl.when(pl.program_id(0) == 0)
    def _():
        db_ref[...] = jnp.zeros_like(db_ref)

    size = f_ref.shape[0]
    same, inherit, same_last, keep = marks(starts, size, count)
    middle = about_middle(size)
    rows, cols = positions(size)
    allowed = (cols <= rows) & same
    after = ((cols >= rows) & same).astype(BF)
    mine = heads * 128
    dz_ref[:, 3 * mine :] = dg_ref[...]
    for k, at in each(heads):
        bound = b_ref[:, at]
        sg, forget, key, a = gates(f_ref[:, at], bound)
        cm = split_dot(middle, a)
        last = cm[size - 1 :]
        mid = jnp.sum(a[: size // 2], axis=0, keepdims=True)
        qz = q_ref[:, at]
        sq = sigmoid(qz)
        up, down = jnp.exp(cm), jnp.exp(-cm)
        v = v_ref[:, at].astype(BF)
        scores, qd, kd = scores_of(qz * sq * up, key * down)
        scores = jnp.where(allowed, scores, 0.0).astype(BF)
        dmix, dmix_low = halves_of(dmix_ref[:, at])
        dscores = jnp.where(allowed, dot_last(dmix, v) + dot_last(dmix_low, v), 0.0).astype(BF)
        enter = enter_ref[k]
        leave = reach(near_ref, far_ref, whole, k)
        leave_low = (leave * jnp.exp(last)).astype(BF)
        enter_low = (enter * jnp.exp(mid)).astype(BF)
        dqd = mm(dscores, kd) + inherit * mm(dmix, enter_low)
        dkd_tail = same_last * mm(v, leave_low)
        dkd = dot_first(dscores, qd) + dkd_tail
        dv = dot_first(scores, dmix) + same_last * dot_last(kd, leave_low)
        qd, kd = qd.astype(F32), kd.astype(F32)
        dlog = dqd * qd - dkd * kd
        rest = jnp.sum(dkd_tail * kd, axis=0, keepdims=True) + keep * jnp.exp(mid + last) * jnp.sum(
            leave * enter, axis=0, keepdims=True
        )
        da = split_dot(after, dlog) + same_last * rest
        dforget = da / forget - dkd * down
        dq = dqd * up * (sq * (1.0 + qz * (1.0 - sq)))
        df = dforget * (1.0 - bound) * sg * (1.0 - sg)
        for n, value in enumerate((df, dv, dq)):
            dz_ref[:, n * mine + 128 * k : n * mine + 128 * (k + 1)] = value.astype(BF)
        db_ref[:, at] += jnp.sum(dforget * (1.0 - sg), axis=0, keepdims=True)


def heads_kernel(heads, order, blocks_ref, *outs):
    for g in range(4):
        here = order[g]
        for n, out_ref in enumerate(outs):
            for k in range(heads):
                to = ((g & 1) * heads + k) * 2 + (g >> 1)
                at = n * heads + k
                out_ref[:, 128 * to : 128 * (to + 1)] = blocks_ref[
                    here, :, 128 * at : 128 * (at + 1)
                ].astype(F32)


def hidden_kernel(chunk, seqs, order, blocks_ref, *outs):
    for g in range(4):
        here = order[g]
        for n, out_ref in enumerate(outs):
            part = blocks_ref[here, :, n * seqs * chunk : (n + 1) * seqs * chunk].astype(F32)
            for j in range(seqs):
                to = (4 * j + g) * chunk
                out_ref[:, to : to + chunk] = part[:, j * chunk : (j + 1) * chunk]


def across(size, width, base=0):
    return pl.BlockSpec((size, width), lambda s, *_: (s, base))


def states(rows, heads):
    return pl.BlockSpec((heads, rows, 128), lambda s, *_: (s, 0, 0))


def fixed(width):
    return pl.BlockSpec((1, width), lambda s, *_: (0, 0))


def call(kernel, grid, scalars, in_specs, out_specs, out_shape, args, flops=1e9):
    params = pltpu.CompilerParams(vmem_limit_bytes=48 * 1024 * 1024)
    return pl.pallas_call(
        kernel,
        grid_spec=pltpu.PrefetchScalarGridSpec(
            num_scalar_prefetch=len(scalars), grid=grid, in_specs=in_specs, out_specs=out_specs
        ),
        out_shape=out_shape,
        compiler_params=params,
        cost_estimate=pl.CostEstimate(flops=int(flops / 100), bytes_accessed=1 << 16, transcendentals=0),
    )(*scalars, *args)


def join(near, far):
    pairs = near.shape[0]
    block = pl.BlockSpec((pairs // 2,) + near.shape[1:], lambda s: (s, 0, 0))
    return call(join_kernel, (2,), (), [block, block], block, jax.ShapeDtypeStruct(near.shape, BF), (near, far))


def equal_halves(tokens):
    return lax.axis_size("seq") * tokens == 2 * MIN_LEN and MIN_LEN == 4 * tokens


def reached(pack, forward, tokens):
    count = lax.axis_size("seq")
    place = lax.axis_index("seq")
    if equal_halves(tokens):
        first = [s for s in range(0, count, 4)]
        order = (0, 1, 2, 3) if forward else (3, 2, 1, 0)

        def hop(value, moves):
            return lax.ppermute(
                value, "seq", [(f + order[a], f + order[b]) for f in first for a, b in moves]
            )

        near = hop(pack, ((0, 1), (2, 3)))
        pair = join(pack, near)
        third = hop(pair, ((1, 3),))
        second = hop(third, ((3, 2),))
        far = jnp.where((place & 3) == order[3], third, second)
        there = (place & 1) == (order[1] & 1)
        return near, far, there.astype(jnp.int32)[None], (pair, third)
    every = lax.all_gather(pack, "seq")
    shape = (pack.shape[0], 128, pack.shape[2])

    def one(k, total):
        at = k if forward else count - 1 - k
        there = lax.dynamic_index_in_dim(every, at, 0, False).astype(F32)
        new = there[:, :128] + there[:, 128:129] * total
        return jnp.where((at < place) if forward else (at > place), new, total)

    total = lax.fori_loop(0, count, one, jnp.zeros(shape, F32))
    total = jnp.concatenate([total, jnp.zeros_like(total[:, :16])], axis=1).astype(BF)
    return total, jnp.zeros_like(total), jnp.ones((1,), jnp.int32), (total, total)


def everywhere(value):
    for axis in ("seq", "dp"):
        bit = 1
        while bit < lax.axis_size(axis):
            pairs = [(s, s ^ bit) for s in range(lax.axis_size(axis))]
            value = value + lax.ppermute(value, axis, pairs)
            bit *= 2
    return value


def shards(
    block_input,
    lengths,
    norm_gain,
    w_q,
    w_f,
    w_i,
    w_g,
    lower_bound,
    group_gain,
    w_o,
    ffn_norm_gain,
    w_gate,
    w_up,
    w_down,
    out_grad,
):
    tokens, width = block_input.shape
    head_dim = group_gain.shape[0]
    heads = width // head_dim // 4
    mine = heads * head_dim
    seqs = lax.axis_size("seq")
    dp = lax.axis_index("dp")
    low_bit, high_bit = dp & 1, dp >> 1

    def of_heads(value, axis):
        shape = value.shape
        cut = value.reshape(shape[:axis] + (2, heads, 2, head_dim) + shape[axis + 1 :])
        cut = lax.dynamic_index_in_dim(cut, high_bit, axis + 2, False)
        cut = lax.dynamic_index_in_dim(cut, low_bit, axis, False)
        return cut.reshape(shape[:axis] + (mine,) + shape[axis + 1 :])

    def to_heads(blocks, axis):
        a, b, c, d = absolute(blocks)
        shape = a.shape
        cut = [v.reshape(shape[:axis] + (heads, head_dim) + shape[axis + 1 :]) for v in (a, b, c, d)]
        pair = [jnp.stack([cut[k], cut[k + 2]], axis=axis + 1) for k in range(2)]
        full = jnp.stack(pair, axis=axis)
        return full.reshape(shape[:axis] + (4 * mine,) + shape[axis + 1 :])

    chunk = w_down.shape[0] // 4
    ff = chunk * seqs

    def of_hidden(value):
        cut = value.reshape(value.shape[0], seqs, 4, chunk)
        return lax.dynamic_index_in_dim(cut, dp, 2, False).reshape(value.shape[0], ff)

    def to_hidden(blocks):
        cut = [v.reshape(v.shape[0], seqs, 1, chunk) for v in absolute(blocks)]
        return jnp.concatenate(cut, axis=2).reshape(blocks[0].shape[0], 4 * ff)

    def gather_seq(value):
        return lax.all_gather(value, "seq", axis=0, tiled=True)

    def scatter_seq(value):
        return lax.psum_scatter(value.astype(BF), "seq", scatter_dimension=0, tiled=True)

    def blocks_dp(value):
        rows = value.shape[0]
        full = gather_dp(value)
        return [full[k * rows : (k + 1) * rows] for k in range(4)]

    w4 = gather_seq(jnp.concatenate([of_heads(w, 1) for w in (w_f, w_i, w_q, w_g)], axis=1))

    x = block_input.astype(F32)
    r1 = lax.rsqrt(jnp.mean(x * x, axis=-1, keepdims=True) + EPS)
    h = (x * r1 * norm_gain).astype(BF)

    starts = jnp.cumsum(lengths[0]) - lengths[0] - lax.axis_index("seq") * tokens
    count = lengths.shape[1]
    if equal_halves(tokens):
        starts = jnp.broadcast_to(starts[None], (4, count))
    else:
        starts = jnp.stack([starts] + [swap(starts, k) for k in (1, 2, 3)])
        h = later(h, starts)
    h_all = gather_dp(h)
    w_o, out_own = later((w_o, out_grad), h_all)
    natural = w_o.shape[0] == 2 * head_dim
    if natural:
        part = lax.dynamic_slice_in_dim(w_o, dp * (head_dim // 2), head_dim // 2, 0)
        wo = gather_seq(part)
    else:
        wo = of_heads(gather_seq(w_o), 0)

    og_all = gather_dp(out_own)
    z = mm(h_all, w4)
    w_gate, w_up = later((w_gate, w_up), h_all)
    wgu = gather_seq(jnp.concatenate([of_hidden(w_gate), of_hidden(w_up)], axis=1))
    w_down = later(w_down, z)
    wd = gather_seq(lax.dynamic_slice_in_dim(w_down, dp * chunk, chunk, 0))

    bound = of_heads(lower_bound, 0)[None]
    gain = group_gain[None]

    grid = (4,)
    pairs = heads * 4
    rows = 4 * tokens
    wide = jax.ShapeDtypeStruct((rows, mine), F32)
    thin = jax.ShapeDtypeStruct((rows, mine), BF)
    packed = jax.ShapeDtypeStruct((pairs, 144, 128), BF)
    one = across(tokens, mine)
    fl, vl, ql, gl = (across(tokens, mine, k) for k in range(4))
    pack_spec, state_spec = states(144, heads), states(128, heads)

    pack = call(
        functools.partial(end_kernel, count, heads), grid, (starts,),
        [fl, vl, fixed(mine)], pack_spec, packed, (z, z, bound), 2e9,
    )
    near, far, whole, _ = reached(pack, True, tokens)
    intra, qs = call(
        functools.partial(intra_kernel, count, heads), grid, (starts,),
        [fl, vl, ql, fixed(mine)], [one, one], [wide, thin], (z, z, z, bound), 3e9,
    )
    if natural:
        halves = later(wo, pack)
        own = lax.dynamic_slice_in_dim(halves, low_bit * (mine // 2), mine // 2, 0)
        give = lax.dynamic_slice_in_dim(halves, (1 - low_bit) * (mine // 2), mine // 2, 0)
        wo = pair_halves(own, swap(give, 1), low_bit, heads)
    mixed, on, enter = call(
        functools.partial(mixed_kernel, heads), grid, (whole,),
        [one, one, gl, fixed(128), pack_spec, pack_spec],
        [one, one, state_spec],
        [wide, thin, jax.ShapeDtypeStruct((pairs, 128, 128), F32)],
        (intra, qs, z, gain, near, far),
    )

    branch = scatter_dp(mm(on, wo, BF))
    branch, og_all = lax.optimization_barrier((branch, og_all))
    y = x + branch
    r2 = lax.rsqrt(jnp.mean(y * y, axis=-1, keepdims=True) + EPS)
    h2_all = gather_dp((y * r2 * ffn_norm_gain).astype(BF))

    gu = mm(h2_all, wgu)
    gate, upper = gu[:, :ff], gu[:, ff:]
    hidden = (silu(gate) * upper).astype(BF)
    down_part = dot_first(hidden, og_all, BF)
    down_rows = scatter_seq(down_part)
    d_hidden = dot_last(og_all, later(wd, down_part))
    d_gate = (d_hidden * upper * silu_grad(gate)).astype(BF)
    d_upper = (d_hidden * silu(gate)).astype(BF)
    d_gu = jnp.concatenate([d_gate, d_upper], axis=1)
    h2_part = dot_last(d_gu, wgu, BF)
    gu_part = dot_first(h2_all, later(d_gu, h2_part), BF)
    gu_rows = scatter_seq(gu_part)
    d_h2 = later(scatter_dp(h2_part), gu_part)

    og = out_grad.astype(F32)
    d_ffn_gain = jnp.sum(d_h2 * y * r2, axis=0)
    u2 = d_h2 * ffn_norm_gain
    d_y = og + r2 * u2 - y * (r2 * r2 * r2) * jnp.mean(u2 * y, axis=-1, keepdims=True)
    d_y_low, down_rows = lax.optimization_barrier((d_y.astype(BF), down_rows))
    out_part = mm(later(hidden, d_y_low), wd, BF)
    d_branch, out_part = lax.optimization_barrier((gather_dp(d_y_low), out_part))

    o_part = dot_first(on, d_branch, BF)
    d_on = dot_last(later(d_branch, o_part), wo)
    d_mixed, d_gz, d_pack, d_gain = call(
        functools.partial(norm_back_kernel, heads), grid, (),
        [one, gl, one, one, fixed(128), pack_spec],
        [one, one, pack_spec, fixed(128)],
        [wide, thin, packed, jax.ShapeDtypeStruct((1, 128), F32)],
        (d_on, z, mixed, qs, gain, pack),
    )
    near, far, whole, passed = reached(d_pack, False, tokens)
    out_part, o_part = later((out_part, o_part), passed[0])
    onward, at_hand = scatter_begin(out_part)
    result = (y + scatter_end(later(onward, passed[1]), at_hand)).astype(BF)

    if natural:
        cut = o_part.reshape(heads, 2, head_dim // 2, width)
        own = lax.dynamic_index_in_dim(cut, low_bit, 1, False).reshape(mine // 2, width)
        give = lax.dynamic_index_in_dim(cut, 1 - low_bit, 1, False).reshape(mine // 2, width)
        got = later(swap(give, 1), result)
        o_full = jnp.where(
            low_bit == 0,
            jnp.concatenate([own, got], axis=0),
            jnp.concatenate([got, own], axis=0),
        )
    else:
        none = jnp.zeros_like(o_part)
        o_full = to_heads([o_part, none, none, none], 0)
    o_rows = scatter_seq(o_full)

    near, far = later((near, far), result, o_full, gu_rows)
    dz, d_bound = call(
        functools.partial(back_kernel, count, heads), grid, (starts, whole),
        [fl, vl, ql, fixed(mine), one, one, state_spec, pack_spec, pack_spec],
        [across(tokens, 4 * mine), fixed(mine)],
        [jax.ShapeDtypeStruct((rows, 4 * mine), BF), jax.ShapeDtypeStruct((1, mine), F32)],
        (z, z, z, bound, d_gz, d_mixed, enter, near, far), 8e9,
    )

    gate_parts, up_parts = gather_parts(gu_rows[:, :ff]), gather_parts(gu_rows[:, ff:])
    fv_part = dot_first(h_all, later(dz, gate_parts[1:3])[:, : 2 * mine], BF)
    fv_rows = scatter_seq(fv_part)
    h_part = dot_last(later(dz, fv_part, up_parts[1:3]), w4, BF)
    d_h = scatter_dp(h_part)
    dz, o_rows = later((dz, o_rows), h_part)
    qg_part = dot_first(h_all, dz[:, 2 * mine :], BF)
    qg_rows = scatter_seq(qg_part)
    fv_rows = later(fv_rows, gate_parts[1:], up_parts[1:], d_h)
    down_parts = gather_parts(later(down_rows, d_h))

    order = jnp.arange(4, dtype=jnp.int32) ^ dp.astype(jnp.int32)

    def whole_rows(parts, kernel, columns, flat):
        part, total = parts[0].shape[0], 4 * columns
        count = parts[0].shape[1] // columns
        blocks = jnp.concatenate(parts, axis=0).reshape(4, part, count * columns)
        if not flat:
            return [to_hidden([blocks[k] for k in range(4)]).astype(F32)]
        tall = min(64, part)
        out = jax.ShapeDtypeStruct((part, total), F32)
        return call(
            kernel, (part // tall,), (order,),
            [pl.BlockSpec((4, tall, count * columns), lambda s, *_: (0, s, 0))],
            [pl.BlockSpec((tall, total), lambda s, *_: (s, 0))] * count, [out] * count, (blocks,),
        )

    if natural:
        grad_o = jnp.concatenate(absolute(blocks_dp(o_rows)), axis=0).astype(F32)
    else:
        grad_o = lax.psum(o_rows.astype(F32), "dp")
    down_all = down_parts[:3] + (jnp.concatenate(down_parts[3:], axis=0),)
    grad_down = jnp.concatenate(absolute(down_all), axis=0).astype(F32)
    join_hidden = functools.partial(hidden_kernel, chunk, seqs)
    [grad_gate] = whole_rows(gate_parts, join_hidden, ff, chunk % 16 == 0)
    [grad_up] = whole_rows(up_parts, join_hidden, ff, chunk % 16 == 0)
    join_heads = functools.partial(heads_kernel, heads)
    grad_f, grad_i = whole_rows(gather_parts(fv_rows), join_heads, mine, True)
    grad_q, grad_g = whole_rows(gather_parts(later(qg_rows, fv_rows)), join_heads, mine, True)

    d_norm_gain = jnp.sum(d_h * x * r1, axis=0)
    u1 = d_h * norm_gain
    d_x = d_y + r1 * u1 - x * (r1 * r1 * r1) * jnp.mean(u1 * x, axis=-1, keepdims=True)

    zero = jnp.zeros((mine,), F32)
    d_bound = to_heads([d_bound[0], zero, zero, zero], 0)
    small = everywhere(jnp.concatenate([d_norm_gain, d_ffn_gain, d_bound, d_gain[0]]))
    return (
        result,
        d_x.astype(BF),
        small[:width],
        grad_q,
        grad_f,
        grad_i,
        grad_g,
        small[2 * width : 3 * width],
        small[3 * width :],
        grad_o,
        small[width : 2 * width],
        grad_gate,
        grad_up,
        grad_down,
    )


def solution(mesh):
    both = P(("dp", "seq"), None)
    rows = P("seq", None)
    return jax.shard_map(
        shards,
        mesh=mesh,
        in_specs=(
            both, P("dp", None), P(), rows, rows, rows, rows, P(), P(), rows, P(), rows, rows, rows, both,
        ),
        out_specs=(
            both, both, P(), rows, rows, rows, rows, P(), P(), rows, P(), rows, rows, rows,
        ),
        check_vma=False,
    )
```

```python
import functools

import jax
import jax.numpy as jnp
from jax import lax
from jax.experimental import pallas as pl
from jax.experimental.pallas import tpu as pltpu
from jax.sharding import PartitionSpec as P

EPS = 1e-06
MIN_LEN = 1024
BF = jnp.bfloat16
F32 = jnp.float32


def sigmoid(value):
    return jax.nn.sigmoid(value)


def silu(value):
    return value * sigmoid(value)


def silu_grad(value):
    s = sigmoid(value)
    return s * (1.0 + value * (1.0 - s))


def mm(left, right, kind=F32):
    return jnp.dot(left, right, preferred_element_type=F32).astype(kind)


def dot_first(left, right, kind=F32):
    return lax.dot_general(
        left, right, (((0,), (0,)), ((), ())), preferred_element_type=F32
    ).astype(kind)


def dot_last(left, right, kind=F32):
    return lax.dot_general(
        left, right, (((1,), (1,)), ((), ())), preferred_element_type=F32
    ).astype(kind)


def swap(value, bits):
    count = lax.axis_size("dp")
    return lax.ppermute(value, "dp", [(s, s ^ bits) for s in range(count)])


def gather_begin(own):
    return own, swap(own, 1), swap(own, 2)


def gather_end(own, one, two):
    half = own.shape[0] // 2
    top, bottom = swap(one[:half], 2), swap(two[half:], 1)
    return own, one, two, top, bottom


def gather_parts(own):
    return gather_end(*gather_begin(own))


def gather_dp(own):
    return jnp.concatenate(gather_parts(own), axis=0)


def scatter_begin(parts):
    rows = parts.shape[0] // 4
    half = rows // 2
    p0, p1, p2, p3 = (parts[k * rows : (k + 1) * rows] for k in range(4))
    top, bottom = swap(p3[:half], 1), swap(p3[half:], 2)
    one_a, two_b = swap(p1[:half], 1), swap(p2[half:], 2)
    two_a = (p2[:half].astype(F32) + top.astype(F32)).astype(BF)
    one_b = (p1[half:].astype(F32) + bottom.astype(F32)).astype(BF)
    return (two_a, one_b), (p0, one_a, two_b)


def scatter_end(onward, at_hand):
    p0, one_a, two_b = at_hand
    two_a, one_b = swap(onward[0], 2), swap(onward[1], 1)
    one = jnp.concatenate([one_a, one_b], axis=0).astype(F32)
    two = jnp.concatenate([two_a, two_b], axis=0).astype(F32)
    return p0.astype(F32) + one + two


def scatter_dp(parts):
    return scatter_end(*scatter_begin(parts))


def later(value, *needed):
    return lax.optimization_barrier((value, needed))[0]


def pair_halves(own, other, place, heads):
    width = own.shape[1]
    own, other = (v.reshape(heads, 1, -1, width) for v in (own, other))
    both = jnp.where(
        place == 0,
        jnp.concatenate([own, other], axis=1),
        jnp.concatenate([other, own], axis=1),
    )
    return both.reshape(-1, width)


def absolute(blocks):
    place = lax.axis_index("dp")
    odd, high = (place & 1) == 1, (place & 2) == 2
    a, b, c, d = blocks
    a, b = jnp.where(odd, b, a), jnp.where(odd, a, b)
    c, d = jnp.where(odd, d, c), jnp.where(odd, c, d)
    return (
        jnp.where(high, c, a),
        jnp.where(high, d, b),
        jnp.where(high, a, c),
        jnp.where(high, b, d),
    )


def marks(starts_ref, size, count):
    slot = pl.program_id(0)
    col = lax.broadcasted_iota(jnp.int32, (size, 1), 0)
    row = lax.broadcasted_iota(jnp.int32, (1, size), 1)
    sid_c = jnp.zeros((size, 1), jnp.int32)
    sid_r = jnp.zeros((1, size), jnp.int32)
    sid_last = jnp.int32(0)
    begun = jnp.zeros((size, 1), jnp.int32)
    ended = jnp.int32(0)
    for j in range(count):
        at = starts_ref[slot, j]
        sid_c += (col >= at).astype(jnp.int32)
        sid_r += (row >= at).astype(jnp.int32)
        sid_last += (size - 1 >= at).astype(jnp.int32)
        begun += ((col >= at) & (at >= 0)).astype(jnp.int32)
        ended += ((size - 1 >= at) & (at >= 0)).astype(jnp.int32)
    inherit = (begun == 0).astype(F32)
    same_last = (sid_c == sid_last).astype(F32)
    keep = (ended == 0).astype(F32)
    return sid_c == sid_r, inherit, same_last, keep


def split_dot(left, value):
    high = value.astype(BF)
    low = (value - high.astype(F32)).astype(BF)
    return mm(left, high) + mm(left, low)


def halves_of(value):
    high = value.astype(BF)
    return high, (value - high.astype(F32)).astype(BF)


def scores_of(qd, kd):
    (qh, ql), (kh, kl) = halves_of(qd), halves_of(kd)
    return dot_last(qh, kh) + (dot_last(qh, kl) + dot_last(ql, kh)), qh, kh


def gates(f, bound):
    sg = sigmoid(f)
    forget = bound + (1.0 - bound) * sg
    return sg, forget, (1.0 - bound) * (1.0 - sg), jnp.log(forget)


def positions(size):
    rows = lax.broadcasted_iota(jnp.int32, (size, size), 0)
    cols = lax.broadcasted_iota(jnp.int32, (size, size), 1)
    return rows, cols


def about_middle(size):
    rows, cols = positions(size)
    return (cols <= rows).astype(BF) - (cols < size // 2).astype(BF)


def each(heads):
    return [(k, slice(128 * k, 128 * (k + 1))) for k in range(heads)]


def end_kernel(count, heads, starts, f_ref, v_ref, b_ref, pack_ref):
    size = f_ref.shape[0]
    _, _, same_last, keep = marks(starts, size, count)
    middle = about_middle(size)
    for k, at in each(heads):
        _, _, key, a = gates(f_ref[:, at], b_ref[:, at])
        cm = split_dot(middle, a)
        total = jnp.sum(a, axis=0, keepdims=True)
        tail = (key * jnp.exp(cm[size - 1 :] - cm) * same_last).astype(BF)
        pack_ref[k, :128] = dot_first(v_ref[:, at].astype(BF), tail).astype(BF)
        pack_ref[k, 128:] = jnp.broadcast_to(jnp.exp(total) * keep, (16, 128)).astype(BF)


def intra_kernel(count, heads, starts, f_ref, v_ref, q_ref, b_ref, out_ref, qs_ref):
    size = f_ref.shape[0]
    same, inherit, _, _ = marks(starts, size, count)
    middle = about_middle(size)
    rows, cols = positions(size)
    allowed = (cols <= rows) & same
    for _, at in each(heads):
        _, _, key, a = gates(f_ref[:, at], b_ref[:, at])
        cm = split_dot(middle, a)
        mid = jnp.sum(a[: size // 2], axis=0, keepdims=True)
        q = silu(q_ref[:, at])
        scores = jnp.where(allowed, scores_of(q * jnp.exp(cm), key * jnp.exp(-cm))[0], 0.0)
        out_ref[:, at] = mm(scores.astype(BF), v_ref[:, at].astype(BF))
        qs_ref[:, at] = (q * jnp.exp(cm + mid) * inherit).astype(BF)


def join_kernel(near_ref, far_ref, out_ref):
    near, far = near_ref[...].astype(F32), far_ref[...].astype(F32)
    decay = near[:, 128:129]
    out_ref[:, :128] = (near[:, :128] + decay * far[:, :128]).astype(BF)
    out_ref[:, 128:] = (near[:, 128:] * far[:, 128:]).astype(BF)


def reach(near_ref, far_ref, whole_ref, k):
    decay = jnp.where(whole_ref[0] == 1, near_ref[k, 128:].astype(F32)[:1], 1.0)
    return near_ref[k, :128].astype(F32) + decay * far_ref[k, :128].astype(F32)


def mixed_kernel(
    heads, whole, out_ref, qs_ref, g_ref, gain_ref, near_ref, far_ref, mixed_ref, on_ref, enter_ref
):
    for k, at in each(heads):
        enter = reach(near_ref, far_ref, whole, k)
        enter_ref[k] = enter
        mixed = out_ref[:, at] + dot_last(qs_ref[:, at], enter.astype(BF))
        mixed_ref[:, at] = mixed
        r = lax.rsqrt(jnp.mean(mixed * mixed, axis=-1, keepdims=True) + EPS)
        on_ref[:, at] = (mixed * r * gain_ref[...] * silu(g_ref[:, at])).astype(BF)


def norm_back_kernel(
    heads, don_ref, g_ref, mixed_ref, qs_ref, gain_ref, pack_ref, dmix_ref, dg_ref, dpack_ref, dgain_ref
):
    @pl.when(pl.program_id(0) == 0)
    def _():
        dgain_ref[...] = jnp.zeros_like(dgain_ref)

    gain = gain_ref[...]
    for k, at in each(heads):
        don, gz, mixed = don_ref[:, at], g_ref[:, at], mixed_ref[:, at]
        sg = sigmoid(gz)
        s = gz * sg
        r = lax.rsqrt(jnp.mean(mixed * mixed, axis=-1, keepdims=True) + EPS)
        n = mixed * r
        w = don * gain * s
        dmix = r * (w - n * jnp.mean(w * n, axis=-1, keepdims=True))
        dmix_ref[:, at] = dmix
        dg_ref[:, at] = (don * gain * n * (sg * (1.0 + gz * (1.0 - sg)))).astype(BF)
        dpack_ref[k, :128] = dot_first(dmix.astype(BF), qs_ref[:, at]).astype(BF)
        dpack_ref[k, 128:] = pack_ref[k, 128:]
        dgain_ref[...] += jnp.sum(don * s * n, axis=0, keepdims=True)


def back_kernel(
    count, heads, starts, whole, f_ref, v_ref, q_ref, b_ref, dg_ref, dmix_ref, enter_ref, near_ref,
    far_ref, dz_ref, db_ref,
):
    @pl.when(pl.program_id(0) == 0)
    def _():
        db_ref[...] = jnp.zeros_like(db_ref)

    size = f_ref.shape[0]
    same, inherit, same_last, keep = marks(starts, size, count)
    middle = about_middle(size)
    rows, cols = positions(size)
    allowed = (cols <= rows) & same
    after = ((cols >= rows) & same).astype(BF)
    mine = heads * 128
    dz_ref[:, 3 * mine :] = dg_ref[...]
    for k, at in each(heads):
        bound = b_ref[:, at]
        sg, forget, key, a = gates(f_ref[:, at], bound)
        cm = split_dot(middle, a)
        last = cm[size - 1 :]
        mid = jnp.sum(a[: size // 2], axis=0, keepdims=True)
        qz = q_ref[:, at]
        sq = sigmoid(qz)
        up, down = jnp.exp(cm), jnp.exp(-cm)
        v = v_ref[:, at].astype(BF)
        scores, qd, kd = scores_of(qz * sq * up, key * down)
        scores = jnp.where(allowed, scores, 0.0).astype(BF)
        dmix, dmix_low = halves_of(dmix_ref[:, at])
        dscores = jnp.where(allowed, dot_last(dmix, v) + dot_last(dmix_low, v), 0.0).astype(BF)
        enter = enter_ref[k]
        leave = reach(near_ref, far_ref, whole, k)
        leave_low = (leave * jnp.exp(last)).astype(BF)
        enter_low = (enter * jnp.exp(mid)).astype(BF)
        dqd = mm(dscores, kd) + inherit * mm(dmix, enter_low)
        dkd_tail = same_last * mm(v, leave_low)
        dkd = dot_first(dscores, qd) + dkd_tail
        dv = dot_first(scores, dmix) + same_last * dot_last(kd, leave_low)
        qd, kd = qd.astype(F32), kd.astype(F32)
        dlog = dqd * qd - dkd * kd
        rest = jnp.sum(dkd_tail * kd, axis=0, keepdims=True) + keep * jnp.exp(mid + last) * jnp.sum(
            leave * enter, axis=0, keepdims=True
        )
        da = split_dot(after, dlog) + same_last * rest
        dforget = da / forget - dkd * down
        dq = dqd * up * (sq * (1.0 + qz * (1.0 - sq)))
        df = dforget * (1.0 - bound) * sg * (1.0 - sg)
        for n, value in enumerate((df, dv, dq)):
            dz_ref[:, n * mine + 128 * k : n * mine + 128 * (k + 1)] = value.astype(BF)
        db_ref[:, at] += jnp.sum(dforget * (1.0 - sg), axis=0, keepdims=True)


def heads_kernel(heads, order, blocks_ref, *outs):
    for g in range(4):
        here = order[g]
        for n, out_ref in enumerate(outs):
            for k in range(heads):
                to = ((g & 1) * heads + k) * 2 + (g >> 1)
                at = n * heads + k
                out_ref[:, 128 * to : 128 * (to + 1)] = blocks_ref[
                    here, :, 128 * at : 128 * (at + 1)
                ].astype(F32)


def hidden_kernel(chunk, seqs, order, blocks_ref, *outs):
    for g in range(4):
        here = order[g]
        for n, out_ref in enumerate(outs):
            part = blocks_ref[here, :, n * seqs * chunk : (n + 1) * seqs * chunk].astype(F32)
            for j in range(seqs):
                to = (4 * j + g) * chunk
                out_ref[:, to : to + chunk] = part[:, j * chunk : (j + 1) * chunk]


def across(size, width, base=0):
    return pl.BlockSpec((size, width), lambda s, *_: (s, base))


def states(rows, heads):
    return pl.BlockSpec((heads, rows, 128), lambda s, *_: (s, 0, 0))


def fixed(width):
    return pl.BlockSpec((1, width), lambda s, *_: (0, 0))


def call(kernel, grid, scalars, in_specs, out_specs, out_shape, args, flops=1e9):
    params = pltpu.CompilerParams(vmem_limit_bytes=48 * 1024 * 1024)
    return pl.pallas_call(
        kernel,
        grid_spec=pltpu.PrefetchScalarGridSpec(
            num_scalar_prefetch=len(scalars), grid=grid, in_specs=in_specs, out_specs=out_specs
        ),
        out_shape=out_shape,
        compiler_params=params,
        cost_estimate=pl.CostEstimate(flops=int(flops / 100), bytes_accessed=1 << 16, transcendentals=0),
    )(*scalars, *args)


def columns_kernel(left_ref, right_ref, out_ref):
    out_ref[...] = mm(left_ref[...], right_ref[...])


def columns(left, right, first, count):
    rows, depth = left.shape
    return call(
        columns_kernel, (count,), (),
        [
            pl.BlockSpec((rows, depth), lambda n: (0, 0)),
            pl.BlockSpec((depth, 256), lambda n: (0, n + first)),
        ],
        pl.BlockSpec((rows, 256), lambda n: (0, n)),
        jax.ShapeDtypeStruct((rows, 256 * count), F32), (left, right), 2e9 * count,
    )


def rows_kernel(left_ref, right_ref, beside_ref, gain_ref, out_ref, sum_ref):
    out = dot_last(left_ref[...], right_ref[...])
    out_ref[...] = out.astype(BF)
    sum_ref[...] = jnp.sum(out * beside_ref[...].astype(F32), axis=0, keepdims=True) / gain_ref[...]


def against_rows(left, right, beside, gain):
    rows, depth = left.shape
    wide = right.shape[0]
    block = pl.BlockSpec((rows, 256), lambda n: (0, n))
    line = pl.BlockSpec((1, 256), lambda n: (0, n))
    return call(
        rows_kernel, (wide // 256,), (),
        [
            pl.BlockSpec((rows, depth), lambda n: (0, 0)),
            pl.BlockSpec((256, depth), lambda n: (n, 0)),
            block,
            line,
        ],
        [block, line],
        [jax.ShapeDtypeStruct((rows, wide), BF), jax.ShapeDtypeStruct((1, wide), F32)],
        (left, right, beside, gain), 8e9,
    )


def join(near, far):
    pairs = near.shape[0]
    block = pl.BlockSpec((pairs // 2,) + near.shape[1:], lambda s: (s, 0, 0))
    return call(join_kernel, (2,), (), [block, block], block, jax.ShapeDtypeStruct(near.shape, BF), (near, far))


def pick_kernel(heads, place, *refs):
    *mats, last, out = refs
    k = pl.program_id(0)
    half, wide = last.shape[0], out.shape[1] - 4 * heads * 128
    for n, mat in enumerate(mats):
        out[:, pl.ds(pl.multiple_of((n * heads + k) * 128, 128), 128)] = mat[...]

    @pl.when(k == 0)
    def _():
        for n in range(4):
            out[half * n : half * (n + 1), 4 * heads * 128 :] = last[:, wide * n : wide * (n + 1)]


def picked(mats, last, heads):
    dp = lax.axis_index("dp")
    place = jnp.stack([(dp & 1) * 2 * heads + (dp >> 1), dp]).astype(jnp.int32)
    rows, width = mats[0].shape
    column = pl.BlockSpec((rows, 128), lambda k, place: (0, place[0] + 2 * k))
    return call(
        functools.partial(pick_kernel, heads), (heads,), (place,),
        [column] * 4 + [pl.BlockSpec((rows // 4, width), lambda k, place: (place[1], 0))],
        pl.BlockSpec((rows, width + width // 4), lambda k, place: (0, 0)),
        jax.ShapeDtypeStruct((rows, width + width // 4), BF), (*mats, last),
    )


def equal_halves(tokens):
    return lax.axis_size("seq") * tokens == 2 * MIN_LEN and MIN_LEN == 4 * tokens


def reached(pack, forward, tokens, beside):
    count = lax.axis_size("seq")
    place = lax.axis_index("seq")
    if equal_halves(tokens):
        first = [s for s in range(0, count, 4)]
        order = (0, 1, 2, 3) if forward else (3, 2, 1, 0)

        def hop(value, moves):
            return lax.ppermute(
                value, "seq", [(f + order[a], f + order[b]) for f in first for a, b in moves]
            )

        near = hop(pack, ((0, 1), (2, 3)))
        pair = join(pack, near)
        third = later(hop(pair, ((1, 3),)), beside(pair))
        second = hop(third, ((3, 2),))
        far = jnp.where((place & 3) == order[3], third, second)
        there = (place & 1) == (order[1] & 1)
        return near, far, there.astype(jnp.int32)[None]
    every = lax.all_gather(pack, "seq")
    shape = (pack.shape[0], 128, pack.shape[2])

    def one(k, total):
        at = k if forward else count - 1 - k
        there = lax.dynamic_index_in_dim(every, at, 0, False).astype(F32)
        new = there[:, :128] + there[:, 128:129] * total
        return jnp.where((at < place) if forward else (at > place), new, total)

    total = lax.fori_loop(0, count, one, jnp.zeros(shape, F32))
    total = jnp.concatenate([total, jnp.zeros_like(total[:, :16])], axis=1).astype(BF)
    total = later(total, beside(total))
    return total, jnp.zeros_like(total), jnp.ones((1,), jnp.int32)


def everywhere(value):
    for axis in ("seq", "dp"):
        bit = 1
        while bit < lax.axis_size(axis):
            pairs = [(s, s ^ bit) for s in range(lax.axis_size(axis))]
            value = value + lax.ppermute(value, axis, pairs)
            bit *= 2
    return value


def shards(
    block_input,
    lengths,
    norm_gain,
    w_q,
    w_f,
    w_i,
    w_g,
    lower_bound,
    group_gain,
    w_o,
    ffn_norm_gain,
    w_gate,
    w_up,
    w_down,
    out_grad,
):
    tokens, width = block_input.shape
    head_dim = group_gain.shape[0]
    heads = width // head_dim // 4
    mine = heads * head_dim
    seqs = lax.axis_size("seq")
    dp = lax.axis_index("dp")
    low_bit, high_bit = dp & 1, dp >> 1

    def of_heads(value, axis):
        shape = value.shape
        cut = value.reshape(shape[:axis] + (2, heads, 2, head_dim) + shape[axis + 1 :])
        cut = lax.dynamic_index_in_dim(cut, high_bit, axis + 2, False)
        cut = lax.dynamic_index_in_dim(cut, low_bit, axis, False)
        return cut.reshape(shape[:axis] + (mine,) + shape[axis + 1 :])

    def to_heads(blocks, axis):
        a, b, c, d = absolute(blocks)
        shape = a.shape
        cut = [v.reshape(shape[:axis] + (heads, head_dim) + shape[axis + 1 :]) for v in (a, b, c, d)]
        pair = [jnp.stack([cut[k], cut[k + 2]], axis=axis + 1) for k in range(2)]
        full = jnp.stack(pair, axis=axis)
        return full.reshape(shape[:axis] + (4 * mine,) + shape[axis + 1 :])

    chunk = w_down.shape[0] // 4
    ff = chunk * seqs

    def of_hidden(value):
        cut = value.reshape(value.shape[0], seqs, 4, chunk)
        return lax.dynamic_index_in_dim(cut, dp, 2, False).reshape(value.shape[0], ff)

    def to_hidden(blocks):
        cut = [v.reshape(v.shape[0], seqs, 1, chunk) for v in absolute(blocks)]
        return jnp.concatenate(cut, axis=2).reshape(blocks[0].shape[0], 4 * ff)

    def gather_seq(value):
        return lax.all_gather(value, "seq", axis=0, tiled=True)

    def scatter_seq(value):
        return lax.psum_scatter(value.astype(BF), "seq", scatter_dimension=0, tiled=True)

    def blocks_dp(value):
        rows = value.shape[0]
        full = gather_dp(value)
        return [full[k * rows : (k + 1) * rows] for k in range(4)]

    natural = w_o.shape[0] == 2 * head_dim
    if natural:
        both = gather_seq(picked((w_f, w_i, w_q, w_g), w_o, heads))
        halves = both[:, width:].reshape(seqs, 4, head_dim // 2, mine)
        halves = halves.transpose(0, 2, 1, 3).reshape(-1, width)
    else:
        both = gather_seq(jnp.concatenate([of_heads(w, 1) for w in (w_f, w_i, w_q, w_g)], axis=1))

    x = block_input.astype(F32)
    r1 = lax.rsqrt(jnp.mean(x * x, axis=-1, keepdims=True) + EPS)
    h = (x * r1 * norm_gain).astype(BF)

    starts = jnp.cumsum(lengths[0]) - lengths[0] - lax.axis_index("seq") * tokens
    count = lengths.shape[1]
    if equal_halves(tokens):
        starts = jnp.broadcast_to(starts[None], (4, count))
    else:
        starts = jnp.stack([starts] + [swap(starts, k) for k in (1, 2, 3)])
        h = later(h, starts)
    h_all = gather_dp(h)
    og_all = gather_dp(later(out_grad, h_all))
    blocks = 2 * mine // 256
    z_fv = columns(h_all, later(both, og_all), 0, blocks)
    w_gate, w_up = later((w_gate, w_up), h_all)
    wgu = gather_seq(jnp.concatenate([of_hidden(w_gate), of_hidden(w_up)], axis=1))
    bound = of_heads(lower_bound, 0)[None]
    gain = group_gain[None]

    grid = (4,)
    pairs = heads * 4
    rows = 4 * tokens
    wide = jax.ShapeDtypeStruct((rows, mine), F32)
    thin = jax.ShapeDtypeStruct((rows, mine), BF)
    packed = jax.ShapeDtypeStruct((pairs, 144, 128), BF)
    one = across(tokens, mine)
    fl, vl = ql, gl = across(tokens, mine, 0), across(tokens, mine, 1)
    pack_spec, state_spec = states(144, heads), states(128, heads)

    pack = call(
        functools.partial(end_kernel, count, heads), grid, (starts,),
        [fl, vl, fixed(mine)], pack_spec, packed, (z_fv, z_fv, bound), 2e9,
    )
    def within(pair):
        if natural:
            own = lax.dynamic_slice_in_dim(halves, low_bit * (mine // 2), mine // 2, 0)
            give = lax.dynamic_slice_in_dim(halves, (1 - low_bit) * (mine // 2), mine // 2, 0)
            give = later(give, pair)
            got = swap(give, 1)
            wo = pair_halves(own, got, low_bit, heads)
        else:
            wo = of_heads(gather_seq(w_o), 0)
            got = give = wo
        z_qg = columns(h_all, later(both, give), blocks, blocks)
        intra, qs = call(
            functools.partial(intra_kernel, count, heads), grid, (starts,),
            [fl, vl, ql, fixed(mine)], [one, one], [wide, thin],
            (z_fv, z_fv, later(z_qg, got), bound), 3e9,
        )
        kept.extend((wo, z_qg, intra, qs))
        return intra

    kept = []
    near, far, whole = reached(pack, True, tokens, within)
    wo, z_qg, intra, qs = kept
    w_down = later(w_down, z_qg)
    wd = gather_seq(lax.dynamic_slice_in_dim(w_down, dp * chunk, chunk, 0))
    mixed, on, enter = call(
        functools.partial(mixed_kernel, heads), grid, (whole,),
        [one, one, gl, fixed(128), pack_spec, pack_spec],
        [one, one, state_spec],
        [wide, thin, jax.ShapeDtypeStruct((pairs, 128, 128), F32)],
        (intra, qs, z_qg, gain, near, far),
    )

    branch = scatter_dp(mm(on, wo, BF))
    y = x + branch
    r2 = lax.rsqrt(jnp.mean(y * y, axis=-1, keepdims=True) + EPS)
    h2_all = gather_dp((y * r2 * ffn_norm_gain).astype(BF))

    gu = mm(h2_all, wgu)
    gate, upper = gu[:, :ff], gu[:, ff:]
    hidden = (silu(gate) * upper).astype(BF)
    down_part = dot_first(hidden, og_all, BF)
    down_rows = scatter_seq(down_part)
    d_hidden = dot_last(og_all, later(wd, down_part))
    d_gate = (d_hidden * upper * silu_grad(gate)).astype(BF)
    d_upper = (d_hidden * silu(gate)).astype(BF)
    d_gu = jnp.concatenate([d_gate, d_upper], axis=1)
    h2_part = dot_last(d_gu, wgu, BF)
    gu_part = dot_first(h2_all, later(d_gu, h2_part), BF)
    gu_rows = scatter_seq(gu_part)
    d_h2 = later(scatter_dp(h2_part), gu_part)

    og = out_grad.astype(F32)
    d_ffn_gain = jnp.sum(d_h2 * y * r2, axis=0)
    u2 = d_h2 * ffn_norm_gain
    d_y = og + r2 * u2 - y * (r2 * r2 * r2) * jnp.mean(u2 * y, axis=-1, keepdims=True)
    d_y_low, down_rows = lax.optimization_barrier((d_y.astype(BF), down_rows))
    out_part = mm(later(hidden, d_y_low), wd, BF)
    d_branch, out_part = lax.optimization_barrier((gather_dp(d_y_low), out_part))

    o_part = dot_first(on, d_branch, BF)
    d_on = dot_last(later(d_branch, o_part), wo)
    d_mixed, d_gz, d_pack, d_gain = call(
        functools.partial(norm_back_kernel, heads), grid, (),
        [one, gl, one, one, fixed(128), pack_spec],
        [one, one, pack_spec, fixed(128)],
        [wide, thin, packed, jax.ShapeDtypeStruct((1, 128), F32)],
        (d_on, z_qg, mixed, qs, gain, pack),
    )
    def moves(pair):
        if natural:
            cut = o_part.reshape(heads, 2, head_dim // 2, width)
            own = lax.dynamic_index_in_dim(cut, low_bit, 1, False).reshape(mine // 2, width)
            give = lax.dynamic_index_in_dim(cut, 1 - low_bit, 1, False).reshape(mine // 2, width)
            got = later(swap(give, 1), pair)
            o_full = jnp.where(
                low_bit == 0,
                jnp.concatenate([own, got], axis=0),
                jnp.concatenate([got, own], axis=0),
            )
        else:
            none = jnp.zeros_like(o_part)
            o_full = got = to_heads([o_part, none, none, none], 0)
        onward, at_hand = scatter_begin(later(out_part, got))
        sent.extend((o_full, onward, at_hand))
        return onward

    sent = []
    near, far, whole = reached(d_pack, False, tokens, moves)
    o_full, onward, at_hand = sent
    o_rows = scatter_seq(o_full)
    result = (y + scatter_end(onward, at_hand)).astype(BF)

    near, far = later((near, far), o_full, gu_rows)
    dz, d_bound = call(
        functools.partial(back_kernel, count, heads), grid, (starts, whole),
        [fl, vl, ql, fixed(mine), one, one, state_spec, pack_spec, pack_spec],
        [across(tokens, 4 * mine), fixed(mine)],
        [jax.ShapeDtypeStruct((rows, 4 * mine), BF), jax.ShapeDtypeStruct((1, mine), F32)],
        (z_fv, z_fv, z_qg, bound, d_gz, d_mixed, enter, near, far), 8e9,
    )

    gate_parts, up_parts = gather_begin(gu_rows[:, :ff]), gather_begin(gu_rows[:, ff:])
    z_part = dot_first(h_all, later(dz, result, gate_parts, up_parts), BF)
    z_rows = scatter_seq(z_part)
    h_part, d_norm_gain = against_rows(later(dz, z_part), both, h_all, norm_gain[None])
    down_parts = gather_begin(later(down_rows, z_part))
    h_part, down_parts = lax.optimization_barrier((h_part, down_parts))
    onward, at_hand = scatter_begin(h_part)
    gate_parts, up_parts, down_parts, o_rows = later((gate_parts, up_parts, down_parts, o_rows), onward)
    gate_parts, up_parts, down_parts = (gather_end(*v) for v in (gate_parts, up_parts, down_parts))
    d_h = scatter_end(onward, at_hand)
    z_rows = later(z_rows, gate_parts, up_parts, down_parts, d_h)

    order = jnp.arange(4, dtype=jnp.int32) ^ dp.astype(jnp.int32)

    def whole_rows(parts, kernel, columns, flat):
        part, total = parts[0].shape[0], 4 * columns
        count = parts[0].shape[1] // columns
        blocks = jnp.concatenate(parts, axis=0).reshape(4, part, count * columns)
        if not flat:
            return [to_hidden([blocks[k] for k in range(4)]).astype(F32)]
        tall = min(64, part)
        out = jax.ShapeDtypeStruct((part, total), F32)
        return call(
            kernel, (part // tall,), (order,),
            [pl.BlockSpec((4, tall, count * columns), lambda s, *_: (0, s, 0))],
            [pl.BlockSpec((tall, total), lambda s, *_: (s, 0))] * count, [out] * count, (blocks,),
        )

    if natural:
        o_parts = gather_parts(o_rows)
        o_all = o_parts[:3] + (jnp.concatenate(o_parts[3:], axis=0),)
        grad_o = jnp.concatenate(absolute(o_all), axis=0).astype(F32)
    else:
        grad_o = lax.psum(o_rows.astype(F32), "dp")
    down_all = down_parts[:3] + (jnp.concatenate(down_parts[3:], axis=0),)
    grad_down = jnp.concatenate(absolute(down_all), axis=0).astype(F32)
    join_hidden = functools.partial(hidden_kernel, chunk, seqs)
    [grad_gate] = whole_rows(gate_parts, join_hidden, ff, chunk % 16 == 0)
    [grad_up] = whole_rows(up_parts, join_hidden, ff, chunk % 16 == 0)
    join_heads = functools.partial(heads_kernel, heads)
    grad_f, grad_i, grad_q, grad_g = whole_rows(gather_parts(z_rows), join_heads, mine, True)

    u1 = d_h * norm_gain
    d_x = d_y + r1 * u1 - x * (r1 * r1 * r1) * jnp.mean(u1 * x, axis=-1, keepdims=True)

    zero = jnp.zeros((mine,), F32)
    d_bound = to_heads([d_bound[0], zero, zero, zero], 0)
    small = jnp.concatenate([d_norm_gain[0], d_ffn_gain, d_bound, d_gain[0]])
    small = everywhere(later(small, onward))
    return (
        result,
        d_x.astype(BF),
        small[:width],
        grad_q,
        grad_f,
        grad_i,
        grad_g,
        small[2 * width : 3 * width],
        small[3 * width :],
        grad_o,
        small[width : 2 * width],
        grad_gate,
        grad_up,
        grad_down,
    )


def solution(mesh):
    both = P(("dp", "seq"), None)
    rows = P("seq", None)
    return jax.shard_map(
        shards,
        mesh=mesh,
        in_specs=(
            both, P("dp", None), P(), rows, rows, rows, rows, P(), P(), rows, P(), rows, rows, rows, both,
        ),
        out_specs=(
            both, both, P(), rows, rows, rows, rows, P(), P(), rows, P(), rows, rows, rows,
        ),
        check_vma=False,
    )
```

```python
import functools

import jax
import jax.numpy as jnp
from jax import lax
from jax.experimental import pallas as pl
from jax.experimental.pallas import tpu as pltpu
from jax.sharding import PartitionSpec as P

EPS = 1e-06
MIN_LEN = 1024
BF = jnp.bfloat16
F32 = jnp.float32


def sigmoid(value):
    return jax.nn.sigmoid(value)


def silu(value):
    return value * sigmoid(value)


def silu_grad(value):
    s = sigmoid(value)
    return s * (1.0 + value * (1.0 - s))


def mm(left, right, kind=F32):
    return jnp.dot(left, right, preferred_element_type=F32).astype(kind)


def dot_first(left, right, kind=F32):
    return lax.dot_general(
        left, right, (((0,), (0,)), ((), ())), preferred_element_type=F32
    ).astype(kind)


def dot_last(left, right, kind=F32):
    return lax.dot_general(
        left, right, (((1,), (1,)), ((), ())), preferred_element_type=F32
    ).astype(kind)


def swap(value, bits):
    count = lax.axis_size("dp")
    return lax.ppermute(value, "dp", [(s, s ^ bits) for s in range(count)])


def gather_begin(own):
    return own, swap(own, 1), swap(own, 2)


def gather_end(own, one, two):
    half = own.shape[0] // 2
    top, bottom = swap(one[:half], 2), swap(two[half:], 1)
    return own, one, two, top, bottom


def gather_parts(own):
    return gather_end(*gather_begin(own))


def gather_dp(own):
    return jnp.concatenate(gather_parts(own), axis=0)


def scatter_begin(parts):
    rows = parts.shape[0] // 4
    half = rows // 2
    p0, p1, p2, p3 = (parts[k * rows : (k + 1) * rows] for k in range(4))
    top, bottom = swap(p3[:half], 1), swap(p3[half:], 2)
    one_a, two_b = swap(p1[:half], 1), swap(p2[half:], 2)
    two_a = (p2[:half].astype(F32) + top.astype(F32)).astype(BF)
    one_b = (p1[half:].astype(F32) + bottom.astype(F32)).astype(BF)
    return (two_a, one_b), (p0, one_a, two_b)


def scatter_end(onward, at_hand):
    p0, one_a, two_b = at_hand
    two_a, one_b = swap(onward[0], 2), swap(onward[1], 1)
    one = jnp.concatenate([one_a, one_b], axis=0).astype(F32)
    two = jnp.concatenate([two_a, two_b], axis=0).astype(F32)
    return p0.astype(F32) + one + two


def scatter_dp(parts):
    return scatter_end(*scatter_begin(parts))


def later(value, *needed):
    return lax.optimization_barrier((value, needed))[0]


def pair_halves(own, other, place, heads):
    width = own.shape[1]
    own, other = (v.reshape(heads, 1, -1, width) for v in (own, other))
    both = jnp.where(
        place == 0,
        jnp.concatenate([own, other], axis=1),
        jnp.concatenate([other, own], axis=1),
    )
    return both.reshape(-1, width)


def absolute(blocks):
    place = lax.axis_index("dp")
    odd, high = (place & 1) == 1, (place & 2) == 2
    a, b, c, d = blocks
    a, b = jnp.where(odd, b, a), jnp.where(odd, a, b)
    c, d = jnp.where(odd, d, c), jnp.where(odd, c, d)
    return (
        jnp.where(high, c, a),
        jnp.where(high, d, b),
        jnp.where(high, a, c),
        jnp.where(high, b, d),
    )


def marks(starts_ref, size, count):
    slot = pl.program_id(0)
    col = lax.broadcasted_iota(jnp.int32, (size, 1), 0)
    row = lax.broadcasted_iota(jnp.int32, (1, size), 1)
    sid_c = jnp.zeros((size, 1), jnp.int32)
    sid_r = jnp.zeros((1, size), jnp.int32)
    sid_last = jnp.int32(0)
    begun = jnp.zeros((size, 1), jnp.int32)
    ended = jnp.int32(0)
    for j in range(count):
        at = starts_ref[slot, j]
        sid_c += (col >= at).astype(jnp.int32)
        sid_r += (row >= at).astype(jnp.int32)
        sid_last += (size - 1 >= at).astype(jnp.int32)
        begun += ((col >= at) & (at >= 0)).astype(jnp.int32)
        ended += ((size - 1 >= at) & (at >= 0)).astype(jnp.int32)
    inherit = (begun == 0).astype(F32)
    same_last = (sid_c == sid_last).astype(F32)
    keep = (ended == 0).astype(F32)
    return sid_c == sid_r, inherit, same_last, keep


def split_dot(left, value):
    high = value.astype(BF)
    low = (value - high.astype(F32)).astype(BF)
    return mm(left, high) + mm(left, low)


def halves_of(value):
    high = value.astype(BF)
    return high, (value - high.astype(F32)).astype(BF)


def scores_of(qd, kd):
    (qh, ql), (kh, kl) = halves_of(qd), halves_of(kd)
    return dot_last(qh, kh) + (dot_last(qh, kl) + dot_last(ql, kh)), qh, kh


def gates(f, bound):
    sg = sigmoid(f)
    forget = bound + (1.0 - bound) * sg
    return sg, forget, (1.0 - bound) * (1.0 - sg), jnp.log(forget)


def positions(size):
    rows = lax.broadcasted_iota(jnp.int32, (size, size), 0)
    cols = lax.broadcasted_iota(jnp.int32, (size, size), 1)
    return rows, cols


def about_middle(size):
    rows, cols = positions(size)
    return (cols <= rows).astype(BF) - (cols < size // 2).astype(BF)


def each(heads):
    return [(k, slice(128 * k, 128 * (k + 1))) for k in range(heads)]


def end_kernel(count, heads, starts, f_ref, v_ref, b_ref, pack_ref):
    size = f_ref.shape[0]
    _, _, same_last, keep = marks(starts, size, count)
    middle = about_middle(size)
    for k, at in each(heads):
        _, _, key, a = gates(f_ref[:, at], b_ref[:, at])
        cm = split_dot(middle, a)
        total = jnp.sum(a, axis=0, keepdims=True)
        tail = (key * jnp.exp(cm[size - 1 :] - cm) * same_last).astype(BF)
        pack_ref[k, :128] = dot_first(v_ref[:, at].astype(BF), tail).astype(BF)
        pack_ref[k, 128:] = jnp.broadcast_to(jnp.exp(total) * keep, (16, 128)).astype(BF)


def intra_kernel(count, heads, starts, f_ref, v_ref, q_ref, b_ref, out_ref, qs_ref):
    size = f_ref.shape[0]
    same, inherit, _, _ = marks(starts, size, count)
    middle = about_middle(size)
    rows, cols = positions(size)
    allowed = (cols <= rows) & same
    for _, at in each(heads):
        _, _, key, a = gates(f_ref[:, at], b_ref[:, at])
        cm = split_dot(middle, a)
        mid = jnp.sum(a[: size // 2], axis=0, keepdims=True)
        q = silu(q_ref[:, at])
        scores = jnp.where(allowed, scores_of(q * jnp.exp(cm), key * jnp.exp(-cm))[0], 0.0)
        out_ref[:, at] = mm(scores.astype(BF), v_ref[:, at].astype(BF))
        qs_ref[:, at] = (q * jnp.exp(cm + mid) * inherit).astype(BF)


def join_kernel(near_ref, far_ref, out_ref):
    near, far = near_ref[...].astype(F32), far_ref[...].astype(F32)
    decay = near[:, 128:129]
    out_ref[:, :128] = (near[:, :128] + decay * far[:, :128]).astype(BF)
    out_ref[:, 128:] = (near[:, 128:] * far[:, 128:]).astype(BF)


def reach(near_ref, far_ref, whole_ref, k):
    decay = jnp.where(whole_ref[0] == 1, near_ref[k, 128:].astype(F32)[:1], 1.0)
    return near_ref[k, :128].astype(F32) + decay * far_ref[k, :128].astype(F32)


def mixed_kernel(
    heads, whole, out_ref, qs_ref, g_ref, gain_ref, near_ref, far_ref, mixed_ref, on_ref, enter_ref
):
    for k, at in each(heads):
        enter = reach(near_ref, far_ref, whole, k)
        enter_ref[k] = enter
        mixed = out_ref[:, at] + dot_last(qs_ref[:, at], enter.astype(BF))
        mixed_ref[:, at] = mixed
        r = lax.rsqrt(jnp.mean(mixed * mixed, axis=-1, keepdims=True) + EPS)
        on_ref[:, at] = (mixed * r * gain_ref[...] * silu(g_ref[:, at])).astype(BF)


def norm_back_kernel(
    heads, don_ref, g_ref, mixed_ref, qs_ref, gain_ref, pack_ref, dmix_ref, dg_ref, dpack_ref, dgain_ref
):
    @pl.when(pl.program_id(0) == 0)
    def _():
        dgain_ref[...] = jnp.zeros_like(dgain_ref)

    gain = gain_ref[...]
    for k, at in each(heads):
        don, gz, mixed = don_ref[:, at], g_ref[:, at], mixed_ref[:, at]
        sg = sigmoid(gz)
        s = gz * sg
        r = lax.rsqrt(jnp.mean(mixed * mixed, axis=-1, keepdims=True) + EPS)
        n = mixed * r
        w = don * gain * s
        dmix = r * (w - n * jnp.mean(w * n, axis=-1, keepdims=True))
        dmix_ref[:, at] = dmix
        dg_ref[:, at] = (don * gain * n * (sg * (1.0 + gz * (1.0 - sg)))).astype(BF)
        dpack_ref[k, :128] = dot_first(dmix.astype(BF), qs_ref[:, at]).astype(BF)
        dpack_ref[k, 128:] = pack_ref[k, 128:]
        dgain_ref[...] += jnp.sum(don * s * n, axis=0, keepdims=True)


def back_kernel(
    count, heads, starts, whole, f_ref, v_ref, q_ref, b_ref, dg_ref, dmix_ref, enter_ref, near_ref,
    far_ref, dz_ref, db_ref,
):
    @pl.when(pl.program_id(0) == 0)
    def _():
        db_ref[...] = jnp.zeros_like(db_ref)

    size = f_ref.shape[0]
    same, inherit, same_last, keep = marks(starts, size, count)
    middle = about_middle(size)
    rows, cols = positions(size)
    allowed = (cols <= rows) & same
    after = ((cols >= rows) & same).astype(BF)
    mine = heads * 128
    dz_ref[:, 3 * mine :] = dg_ref[...]
    for k, at in each(heads):
        bound = b_ref[:, at]
        sg, forget, key, a = gates(f_ref[:, at], bound)
        cm = split_dot(middle, a)
        last = cm[size - 1 :]
        mid = jnp.sum(a[: size // 2], axis=0, keepdims=True)
        qz = q_ref[:, at]
        sq = sigmoid(qz)
        up, down = jnp.exp(cm), jnp.exp(-cm)
        v = v_ref[:, at].astype(BF)
        scores, qd, kd = scores_of(qz * sq * up, key * down)
        scores = jnp.where(allowed, scores, 0.0).astype(BF)
        dmix, dmix_low = halves_of(dmix_ref[:, at])
        dscores = jnp.where(allowed, dot_last(dmix, v) + dot_last(dmix_low, v), 0.0).astype(BF)
        enter = enter_ref[k]
        leave = reach(near_ref, far_ref, whole, k)
        leave_low = (leave * jnp.exp(last)).astype(BF)
        enter_low = (enter * jnp.exp(mid)).astype(BF)
        dqd = mm(dscores, kd) + inherit * mm(dmix, enter_low)
        dkd_tail = same_last * mm(v, leave_low)
        dkd = dot_first(dscores, qd) + dkd_tail
        dv = dot_first(scores, dmix) + same_last * dot_last(kd, leave_low)
        qd, kd = qd.astype(F32), kd.astype(F32)
        dlog = dqd * qd - dkd * kd
        rest = jnp.sum(dkd_tail * kd, axis=0, keepdims=True) + keep * jnp.exp(mid + last) * jnp.sum(
            leave * enter, axis=0, keepdims=True
        )
        da = split_dot(after, dlog) + same_last * rest
        dforget = da / forget - dkd * down
        dq = dqd * up * (sq * (1.0 + qz * (1.0 - sq)))
        df = dforget * (1.0 - bound) * sg * (1.0 - sg)
        for n, value in enumerate((df, dv, dq)):
            dz_ref[:, n * mine + 128 * k : n * mine + 128 * (k + 1)] = value.astype(BF)
        db_ref[:, at] += jnp.sum(dforget * (1.0 - sg), axis=0, keepdims=True)


def heads_kernel(heads, order, blocks_ref, *outs):
    for g in range(4):
        here = order[g]
        for n, out_ref in enumerate(outs):
            for k in range(heads):
                to = ((g & 1) * heads + k) * 2 + (g >> 1)
                at = n * heads + k
                out_ref[:, 128 * to : 128 * (to + 1)] = blocks_ref[
                    here, :, 128 * at : 128 * (at + 1)
                ].astype(F32)


def hidden_kernel(chunk, seqs, order, blocks_ref, *outs):
    for g in range(4):
        here = order[g]
        for n, out_ref in enumerate(outs):
            part = blocks_ref[here, :, n * seqs * chunk : (n + 1) * seqs * chunk].astype(F32)
            for j in range(seqs):
                to = (4 * j + g) * chunk
                out_ref[:, to : to + chunk] = part[:, j * chunk : (j + 1) * chunk]


def across(size, width, base=0):
    return pl.BlockSpec((size, width), lambda s, *_: (s, base))


def states(rows, heads):
    return pl.BlockSpec((heads, rows, 128), lambda s, *_: (s, 0, 0))


def fixed(width):
    return pl.BlockSpec((1, width), lambda s, *_: (0, 0))


def call(kernel, grid, scalars, in_specs, out_specs, out_shape, args, flops=1e9, vmem=48):
    params = pltpu.CompilerParams(vmem_limit_bytes=vmem * 1024 * 1024)
    return pl.pallas_call(
        kernel,
        grid_spec=pltpu.PrefetchScalarGridSpec(
            num_scalar_prefetch=len(scalars), grid=grid, in_specs=in_specs, out_specs=out_specs
        ),
        out_shape=out_shape,
        compiler_params=params,
        cost_estimate=pl.CostEstimate(flops=int(flops / 100), bytes_accessed=1 << 16, transcendentals=0),
    )(*scalars, *args)


def columns_kernel(left_ref, right_ref, out_ref):
    out_ref[...] = mm(left_ref[...], right_ref[...])


def columns(left, right, first, count):
    rows, depth = left.shape
    return call(
        columns_kernel, (count,), (),
        [
            pl.BlockSpec((rows, depth), lambda n: (0, 0)),
            pl.BlockSpec((depth, 256), lambda n: (0, n + first)),
        ],
        pl.BlockSpec((rows, 256), lambda n: (0, n)),
        jax.ShapeDtypeStruct((rows, 256 * count), F32), (left, right), 2e9 * count,
    )


def rows_kernel(left_ref, right_ref, beside_ref, gain_ref, out_ref, sum_ref):
    out = dot_last(left_ref[...], right_ref[...])
    out_ref[...] = out.astype(BF)
    sum_ref[...] = jnp.sum(out * beside_ref[...].astype(F32), axis=0, keepdims=True) / gain_ref[...]


def against_rows(left, right, beside, gain):
    rows, depth = left.shape
    wide = right.shape[0]
    block = pl.BlockSpec((rows, 256), lambda n: (0, n))
    line = pl.BlockSpec((1, 256), lambda n: (0, n))
    return call(
        rows_kernel, (wide // 256,), (),
        [
            pl.BlockSpec((rows, depth), lambda n: (0, 0)),
            pl.BlockSpec((256, depth), lambda n: (n, 0)),
            block,
            line,
        ],
        [block, line],
        [jax.ShapeDtypeStruct((rows, wide), BF), jax.ShapeDtypeStruct((1, wide), F32)],
        (left, right, beside, gain), 8e9,
    )


def join(near, far):
    pairs = near.shape[0]
    block = pl.BlockSpec((pairs // 2,) + near.shape[1:], lambda s: (s, 0, 0))
    return call(join_kernel, (2,), (), [block, block], block, jax.ShapeDtypeStruct(near.shape, BF), (near, far))


def pick_kernel(heads, place, *refs):
    *mats, last, out = refs
    k = pl.program_id(0)
    half, wide = last.shape[0], out.shape[1] - 4 * heads * 128
    for n, mat in enumerate(mats):
        out[:, pl.ds(pl.multiple_of((n * heads + k) * 128, 128), 128)] = mat[...]

    @pl.when(k == 0)
    def _():
        for n in range(4):
            out[half * n : half * (n + 1), 4 * heads * 128 :] = last[:, wide * n : wide * (n + 1)]


def picked(mats, last, heads):
    dp = lax.axis_index("dp")
    place = jnp.stack([(dp & 1) * 2 * heads + (dp >> 1), dp]).astype(jnp.int32)
    rows, width = mats[0].shape
    column = pl.BlockSpec((rows, 128), lambda k, place: (0, place[0] + 2 * k))
    return call(
        functools.partial(pick_kernel, heads), (heads,), (place,),
        [column] * 4 + [pl.BlockSpec((rows // 4, width), lambda k, place: (place[1], 0))],
        pl.BlockSpec((rows, width + width // 4), lambda k, place: (0, 0)),
        jax.ShapeDtypeStruct((rows, width + width // 4), BF), (*mats, last), vmem=62,
    )


def equal_halves(tokens):
    return lax.axis_size("seq") * tokens == 2 * MIN_LEN and MIN_LEN == 4 * tokens


def reached(pack, forward, tokens, beside):
    count = lax.axis_size("seq")
    place = lax.axis_index("seq")
    if equal_halves(tokens):
        first = [s for s in range(0, count, 4)]
        order = (0, 1, 2, 3) if forward else (3, 2, 1, 0)

        def hop(value, moves):
            return lax.ppermute(
                value, "seq", [(f + order[a], f + order[b]) for f in first for a, b in moves]
            )

        near = hop(pack, ((0, 1), (2, 3)))
        pair = join(pack, near)
        third = later(hop(pair, ((1, 3),)), beside(pair))
        second = hop(third, ((3, 2),))
        far = jnp.where((place & 3) == order[3], third, second)
        there = (place & 1) == (order[1] & 1)
        return near, far, there.astype(jnp.int32)[None]
    every = lax.all_gather(pack, "seq")
    shape = (pack.shape[0], 128, pack.shape[2])

    def one(k, total):
        at = k if forward else count - 1 - k
        there = lax.dynamic_index_in_dim(every, at, 0, False).astype(F32)
        new = there[:, :128] + there[:, 128:129] * total
        return jnp.where((at < place) if forward else (at > place), new, total)

    total = lax.fori_loop(0, count, one, jnp.zeros(shape, F32))
    total = jnp.concatenate([total, jnp.zeros_like(total[:, :16])], axis=1).astype(BF)
    total = later(total, beside(total))
    return total, jnp.zeros_like(total), jnp.ones((1,), jnp.int32)


def everywhere(value):
    for axis in ("seq", "dp"):
        bit = 1
        while bit < lax.axis_size(axis):
            pairs = [(s, s ^ bit) for s in range(lax.axis_size(axis))]
            value = value + lax.ppermute(value, axis, pairs)
            bit *= 2
    return value


def shards(
    block_input,
    lengths,
    norm_gain,
    w_q,
    w_f,
    w_i,
    w_g,
    lower_bound,
    group_gain,
    w_o,
    ffn_norm_gain,
    w_gate,
    w_up,
    w_down,
    out_grad,
):
    tokens, width = block_input.shape
    head_dim = group_gain.shape[0]
    heads = width // head_dim // 4
    mine = heads * head_dim
    seqs = lax.axis_size("seq")
    dp = lax.axis_index("dp")
    low_bit, high_bit = dp & 1, dp >> 1

    def of_heads(value, axis):
        shape = value.shape
        cut = value.reshape(shape[:axis] + (2, heads, 2, head_dim) + shape[axis + 1 :])
        cut = lax.dynamic_index_in_dim(cut, high_bit, axis + 2, False)
        cut = lax.dynamic_index_in_dim(cut, low_bit, axis, False)
        return cut.reshape(shape[:axis] + (mine,) + shape[axis + 1 :])

    def to_heads(blocks, axis):
        a, b, c, d = absolute(blocks)
        shape = a.shape
        cut = [v.reshape(shape[:axis] + (heads, head_dim) + shape[axis + 1 :]) for v in (a, b, c, d)]
        pair = [jnp.stack([cut[k], cut[k + 2]], axis=axis + 1) for k in range(2)]
        full = jnp.stack(pair, axis=axis)
        return full.reshape(shape[:axis] + (4 * mine,) + shape[axis + 1 :])

    chunk = w_down.shape[0] // 4
    ff = chunk * seqs

    def of_hidden(value):
        cut = value.reshape(value.shape[0], seqs, 4, chunk)
        return lax.dynamic_index_in_dim(cut, dp, 2, False).reshape(value.shape[0], ff)

    def to_hidden(blocks):
        cut = [v.reshape(v.shape[0], seqs, 1, chunk) for v in absolute(blocks)]
        return jnp.concatenate(cut, axis=2).reshape(blocks[0].shape[0], 4 * ff)

    def gather_seq(value):
        return lax.all_gather(value, "seq", axis=0, tiled=True)

    def scatter_seq(value):
        return lax.psum_scatter(value.astype(BF), "seq", scatter_dimension=0, tiled=True)

    def blocks_dp(value):
        rows = value.shape[0]
        full = gather_dp(value)
        return [full[k * rows : (k + 1) * rows] for k in range(4)]

    natural = w_o.shape[0] == 2 * head_dim
    if natural:
        both = gather_seq(picked((w_f, w_i, w_q, w_g), w_o, heads))
        halves = both[:, width:].reshape(seqs, 4, head_dim // 2, mine)
        halves = halves.transpose(0, 2, 1, 3).reshape(-1, width)
    else:
        both = gather_seq(jnp.concatenate([of_heads(w, 1) for w in (w_f, w_i, w_q, w_g)], axis=1))

    x = block_input.astype(F32)
    r1 = lax.rsqrt(jnp.mean(x * x, axis=-1, keepdims=True) + EPS)
    h = (x * r1 * norm_gain).astype(BF)

    starts = jnp.cumsum(lengths[0]) - lengths[0] - lax.axis_index("seq") * tokens
    count = lengths.shape[1]
    if equal_halves(tokens):
        starts = jnp.broadcast_to(starts[None], (4, count))
    else:
        starts = jnp.stack([starts] + [swap(starts, k) for k in (1, 2, 3)])
        h = later(h, starts)
    h_all = gather_dp(h)
    og_all = gather_dp(later(out_grad, h_all))
    blocks = 2 * mine // 256
    z_fv = columns(h_all, later(both, og_all), 0, blocks)
    w_gate, w_up = later((w_gate, w_up), h_all)
    wgu = gather_seq(jnp.concatenate([of_hidden(w_gate), of_hidden(w_up)], axis=1))
    bound = of_heads(lower_bound, 0)[None]
    gain = group_gain[None]

    grid = (4,)
    pairs = heads * 4
    rows = 4 * tokens
    wide = jax.ShapeDtypeStruct((rows, mine), F32)
    thin = jax.ShapeDtypeStruct((rows, mine), BF)
    packed = jax.ShapeDtypeStruct((pairs, 144, 128), BF)
    one = across(tokens, mine)
    fl, vl = ql, gl = across(tokens, mine, 0), across(tokens, mine, 1)
    pack_spec, state_spec = states(144, heads), states(128, heads)

    pack = call(
        functools.partial(end_kernel, count, heads), grid, (starts,),
        [fl, vl, fixed(mine)], pack_spec, packed, (z_fv, z_fv, bound), 2e9,
    )
    def within(pair):
        if natural:
            own = lax.dynamic_slice_in_dim(halves, low_bit * (mine // 2), mine // 2, 0)
            give = lax.dynamic_slice_in_dim(halves, (1 - low_bit) * (mine // 2), mine // 2, 0)
            give = later(give, pair)
            wo = pair_halves(own, swap(give, 1), low_bit, heads)
        else:
            wo = of_heads(gather_seq(w_o), 0)
            give = wo
        z_qg = columns(h_all, later(both, give), blocks, blocks)
        intra, qs = call(
            functools.partial(intra_kernel, count, heads), grid, (starts,),
            [fl, vl, ql, fixed(mine)], [one, one], [wide, thin],
            (z_fv, z_fv, z_qg, bound), 3e9,
        )
        kept.extend((wo, z_qg, intra, qs))
        return intra

    kept = []
    near, far, whole = reached(pack, True, tokens, within)
    wo, z_qg, intra, qs = kept
    w_down = later(w_down, z_qg)
    wd = gather_seq(lax.dynamic_slice_in_dim(w_down, dp * chunk, chunk, 0))
    mixed, on, enter = call(
        functools.partial(mixed_kernel, heads), grid, (whole,),
        [one, one, gl, fixed(128), pack_spec, pack_spec],
        [one, one, state_spec],
        [wide, thin, jax.ShapeDtypeStruct((pairs, 128, 128), F32)],
        (intra, qs, z_qg, gain, near, far),
    )

    branch = scatter_dp(mm(on, wo, BF))
    y = x + branch
    r2 = lax.rsqrt(jnp.mean(y * y, axis=-1, keepdims=True) + EPS)
    h2_all = gather_dp((y * r2 * ffn_norm_gain).astype(BF))

    gu = mm(h2_all, wgu)
    gate, upper = gu[:, :ff], gu[:, ff:]
    hidden = (silu(gate) * upper).astype(BF)
    down_part = dot_first(hidden, og_all, BF)
    down_rows = scatter_seq(down_part)
    d_hidden = dot_last(og_all, later(wd, down_part))
    d_gate = (d_hidden * upper * silu_grad(gate)).astype(BF)
    d_upper = (d_hidden * silu(gate)).astype(BF)
    d_gu = jnp.concatenate([d_gate, d_upper], axis=1)
    h2_part = dot_last(d_gu, wgu, BF)
    gu_part = dot_first(h2_all, later(d_gu, h2_part), BF)
    gu_rows = scatter_seq(gu_part)
    d_h2 = later(scatter_dp(h2_part), gu_part)

    og = out_grad.astype(F32)
    d_ffn_gain = jnp.sum(d_h2 * y * r2, axis=0)
    u2 = d_h2 * ffn_norm_gain
    d_y = og + r2 * u2 - y * (r2 * r2 * r2) * jnp.mean(u2 * y, axis=-1, keepdims=True)
    d_y_low, down_rows = lax.optimization_barrier((d_y.astype(BF), down_rows))
    out_part = mm(later(hidden, d_y_low), wd, BF)
    d_branch, out_part = lax.optimization_barrier((gather_dp(d_y_low), out_part))

    o_part = dot_first(on, d_branch, BF)
    d_on = dot_last(later(d_branch, o_part), wo)
    d_mixed, d_gz, d_pack, d_gain = call(
        functools.partial(norm_back_kernel, heads), grid, (),
        [one, gl, one, one, fixed(128), pack_spec],
        [one, one, pack_spec, fixed(128)],
        [wide, thin, packed, jax.ShapeDtypeStruct((1, 128), F32)],
        (d_on, z_qg, mixed, qs, gain, pack), 1e13,
    )
    def moves(pair):
        if natural:
            cut = o_part.reshape(heads, 2, head_dim // 2, width)
            own = lax.dynamic_index_in_dim(cut, low_bit, 1, False).reshape(mine // 2, width)
            give = lax.dynamic_index_in_dim(cut, 1 - low_bit, 1, False).reshape(mine // 2, width)
            got = later(swap(give, 1), pair)
            o_full = jnp.where(
                low_bit == 0,
                jnp.concatenate([own, got], axis=0),
                jnp.concatenate([got, own], axis=0),
            )
        else:
            none = jnp.zeros_like(o_part)
            o_full = got = to_heads([o_part, none, none, none], 0)
        onward, at_hand = scatter_begin(later(out_part, got))
        sent.extend((o_full, onward, at_hand))
        return onward

    sent = []
    near, far, whole = reached(d_pack, False, tokens, moves)
    o_full, onward, at_hand = sent
    o_rows = scatter_seq(o_full)
    result = (y + scatter_end(onward, at_hand)).astype(BF)

    near, far = later((near, far), o_full, result)
    dz, d_bound = call(
        functools.partial(back_kernel, count, heads), grid, (starts, whole),
        [fl, vl, ql, fixed(mine), one, one, state_spec, pack_spec, pack_spec],
        [across(tokens, 4 * mine), fixed(mine)],
        [jax.ShapeDtypeStruct((rows, 4 * mine), BF), jax.ShapeDtypeStruct((1, mine), F32)],
        (z_fv, z_fv, z_qg, bound, d_gz, d_mixed, enter, near, far), 8e9,
    )

    gu_parts = gather_begin(later(gu_rows, result))
    z_part = dot_first(h_all, later(dz, result, gu_parts), BF)
    z_rows = scatter_seq(z_part)
    h_part, d_norm_gain = against_rows(later(dz, z_part), both, h_all, norm_gain[None])
    down_parts = gather_begin(later(down_rows, z_part))
    h_part, down_parts = lax.optimization_barrier((h_part, down_parts))
    onward, at_hand = scatter_begin(h_part)
    gu_parts, down_parts = later((gu_parts, down_parts), onward)
    gu_parts, down_parts = gather_end(*gu_parts), gather_end(*down_parts)
    d_h = scatter_end(onward, at_hand)

    zero = jnp.zeros((mine,), F32)
    d_bound = to_heads([d_bound[0], zero, zero, zero], 0)
    small = jnp.concatenate([d_norm_gain[0], d_ffn_gain, d_bound, d_gain[0]])
    small, o_rows = later((small, o_rows), d_h)
    small = everywhere(small)
    if natural:
        o_all = (o_rows, swap(o_rows, 1), swap(o_rows, 2), swap(o_rows, 3))
        grad_o = jnp.concatenate(absolute(o_all), axis=0).astype(F32)
    else:
        o_all = ()
        grad_o = lax.psum(o_rows.astype(F32), "dp")
    z_rows = later(z_rows, gu_parts, down_parts, d_h, small, o_all)

    order = jnp.arange(4, dtype=jnp.int32) ^ dp.astype(jnp.int32)

    def whole_rows(parts, kernel, columns, flat):
        part, total = parts[0].shape[0], 4 * columns
        count = parts[0].shape[1] // columns
        blocks = jnp.concatenate(parts, axis=0).reshape(4, part, count * columns)
        if not flat:
            cut = [blocks[k] for k in range(4)]
            return [
                to_hidden([v[:, k * columns : (k + 1) * columns] for v in cut]).astype(F32)
                for k in range(count)
            ]
        tall = min(64, part)
        out = jax.ShapeDtypeStruct((part, total), F32)
        return call(
            kernel, (part // tall,), (order,),
            [pl.BlockSpec((4, tall, count * columns), lambda s, *_: (0, s, 0))],
            [pl.BlockSpec((tall, total), lambda s, *_: (s, 0))] * count, [out] * count, (blocks,),
        )

    down_all = down_parts[:3] + (jnp.concatenate(down_parts[3:], axis=0),)
    grad_down = jnp.concatenate(absolute(down_all), axis=0).astype(F32)
    join_hidden = functools.partial(hidden_kernel, chunk, seqs)
    grad_gate, grad_up = whole_rows(gu_parts, join_hidden, ff, chunk % 16 == 0)
    join_heads = functools.partial(heads_kernel, heads)
    grad_f, grad_i, grad_q, grad_g = whole_rows(gather_parts(z_rows), join_heads, mine, True)

    u1 = d_h * norm_gain
    d_x = d_y + r1 * u1 - x * (r1 * r1 * r1) * jnp.mean(u1 * x, axis=-1, keepdims=True)

    return (
        result,
        d_x.astype(BF),
        small[:width],
        grad_q,
        grad_f,
        grad_i,
        grad_g,
        small[2 * width : 3 * width],
        small[3 * width :],
        grad_o,
        small[width : 2 * width],
        grad_gate,
        grad_up,
        grad_down,
    )


def solution(mesh):
    both = P(("dp", "seq"), None)
    rows = P("seq", None)
    return jax.shard_map(
        shards,
        mesh=mesh,
        in_specs=(
            both, P("dp", None), P(), rows, rows, rows, rows, P(), P(), rows, P(), rows, rows, rows, both,
        ),
        out_specs=(
            both, both, P(), rows, rows, rows, rows, P(), P(), rows, P(), rows, rows, rows,
        ),
        check_vma=False,
    )
```

```python
import functools

import jax
import jax.numpy as jnp
from jax import lax
from jax.experimental import pallas as pl
from jax.experimental.pallas import tpu as pltpu
from jax.sharding import PartitionSpec as P

EPS = 1e-06
MIN_LEN = 1024
BF = jnp.bfloat16
F32 = jnp.float32


def sigmoid(value):
    return jax.nn.sigmoid(value)


def silu(value):
    return value * sigmoid(value)


def silu_grad(value):
    s = sigmoid(value)
    return s * (1.0 + value * (1.0 - s))


def mm(left, right, kind=F32):
    return jnp.dot(left, right, preferred_element_type=F32).astype(kind)


def dot_first(left, right, kind=F32):
    return lax.dot_general(
        left, right, (((0,), (0,)), ((), ())), preferred_element_type=F32
    ).astype(kind)


def dot_last(left, right, kind=F32):
    return lax.dot_general(
        left, right, (((1,), (1,)), ((), ())), preferred_element_type=F32
    ).astype(kind)


def swap(value, bits):
    count = lax.axis_size("dp")
    return lax.ppermute(value, "dp", [(s, s ^ bits) for s in range(count)])


def gather_begin(own):
    return own, swap(own, 1), swap(own, 2)


def gather_end(own, one, two):
    half = own.shape[0] // 2
    top, bottom = swap(one[:half], 2), swap(two[half:], 1)
    return own, one, two, top, bottom


def gather_parts(own):
    return gather_end(*gather_begin(own))


def gather_dp(own):
    return jnp.concatenate(gather_parts(own), axis=0)


def scatter_begin(parts):
    rows = parts.shape[0] // 4
    half = rows // 2
    p0, p1, p2, p3 = (parts[k * rows : (k + 1) * rows] for k in range(4))
    top, bottom = swap(p3[:half], 1), swap(p3[half:], 2)
    one_a, two_b = swap(p1[:half], 1), swap(p2[half:], 2)
    two_a = (p2[:half].astype(F32) + top.astype(F32)).astype(BF)
    one_b = (p1[half:].astype(F32) + bottom.astype(F32)).astype(BF)
    return (two_a, one_b), (p0, one_a, two_b)


def scatter_end(onward, at_hand):
    p0, one_a, two_b = at_hand
    two_a, one_b = swap(onward[0], 2), swap(onward[1], 1)
    one = jnp.concatenate([one_a, one_b], axis=0).astype(F32)
    two = jnp.concatenate([two_a, two_b], axis=0).astype(F32)
    return p0.astype(F32) + one + two


def scatter_dp(parts):
    return scatter_end(*scatter_begin(parts))


def later(value, *needed):
    return lax.optimization_barrier((value, needed))[0]


def pair_halves(own, other, place, heads):
    width = own.shape[1]
    own, other = (v.reshape(heads, 1, -1, width) for v in (own, other))
    both = jnp.where(
        place == 0,
        jnp.concatenate([own, other], axis=1),
        jnp.concatenate([other, own], axis=1),
    )
    return both.reshape(-1, width)


def absolute(blocks):
    place = lax.axis_index("dp")
    odd, high = (place & 1) == 1, (place & 2) == 2
    a, b, c, d = blocks
    a, b = jnp.where(odd, b, a), jnp.where(odd, a, b)
    c, d = jnp.where(odd, d, c), jnp.where(odd, c, d)
    return (
        jnp.where(high, c, a),
        jnp.where(high, d, b),
        jnp.where(high, a, c),
        jnp.where(high, b, d),
    )


def marks(starts_ref, size, count):
    slot = pl.program_id(0)
    col = lax.broadcasted_iota(jnp.int32, (size, 1), 0)
    row = lax.broadcasted_iota(jnp.int32, (1, size), 1)
    sid_c = jnp.zeros((size, 1), jnp.int32)
    sid_r = jnp.zeros((1, size), jnp.int32)
    sid_last = jnp.int32(0)
    begun = jnp.zeros((size, 1), jnp.int32)
    ended = jnp.int32(0)
    for j in range(count):
        at = starts_ref[slot, j]
        sid_c += (col >= at).astype(jnp.int32)
        sid_r += (row >= at).astype(jnp.int32)
        sid_last += (size - 1 >= at).astype(jnp.int32)
        begun += ((col >= at) & (at >= 0)).astype(jnp.int32)
        ended += ((size - 1 >= at) & (at >= 0)).astype(jnp.int32)
    inherit = (begun == 0).astype(F32)
    same_last = (sid_c == sid_last).astype(F32)
    keep = (ended == 0).astype(F32)
    return sid_c == sid_r, inherit, same_last, keep


def split_dot(left, value):
    high = value.astype(BF)
    low = (value - high.astype(F32)).astype(BF)
    return mm(left, high) + mm(left, low)


def halves_of(value):
    high = value.astype(BF)
    return high, (value - high.astype(F32)).astype(BF)


def scores_of(qd, kd):
    (qh, ql), (kh, kl) = halves_of(qd), halves_of(kd)
    return dot_last(qh, kh) + (dot_last(qh, kl) + dot_last(ql, kh)), qh, kh


def gates(f, bound):
    sg = sigmoid(f)
    forget = bound + (1.0 - bound) * sg
    return sg, forget, (1.0 - bound) * (1.0 - sg), jnp.log(forget)


def positions(size):
    rows = lax.broadcasted_iota(jnp.int32, (size, size), 0)
    cols = lax.broadcasted_iota(jnp.int32, (size, size), 1)
    return rows, cols


def about_middle(size):
    rows, cols = positions(size)
    return (cols <= rows).astype(BF) - (cols < size // 2).astype(BF)


def each(heads):
    return [(k, slice(128 * k, 128 * (k + 1))) for k in range(heads)]


def end_kernel(count, heads, starts, f_ref, v_ref, b_ref, pack_ref):
    size = f_ref.shape[0]
    _, _, same_last, keep = marks(starts, size, count)
    middle = about_middle(size)
    for k, at in each(heads):
        _, _, key, a = gates(f_ref[:, at], b_ref[:, at])
        cm = split_dot(middle, a)
        total = jnp.sum(a, axis=0, keepdims=True)
        tail = (key * jnp.exp(cm[size - 1 :] - cm) * same_last).astype(BF)
        pack_ref[k, :128] = dot_first(v_ref[:, at].astype(BF), tail).astype(BF)
        pack_ref[k, 128:] = jnp.broadcast_to(jnp.exp(total) * keep, (16, 128)).astype(BF)


def intra_kernel(count, heads, starts, f_ref, v_ref, q_ref, b_ref, out_ref, qs_ref):
    size = f_ref.shape[0]
    same, inherit, _, _ = marks(starts, size, count)
    middle = about_middle(size)
    rows, cols = positions(size)
    allowed = (cols <= rows) & same
    for _, at in each(heads):
        _, _, key, a = gates(f_ref[:, at], b_ref[:, at])
        cm = split_dot(middle, a)
        mid = jnp.sum(a[: size // 2], axis=0, keepdims=True)
        q = silu(q_ref[:, at])
        scores = jnp.where(allowed, scores_of(q * jnp.exp(cm), key * jnp.exp(-cm))[0], 0.0)
        out_ref[:, at] = mm(scores.astype(BF), v_ref[:, at].astype(BF))
        qs_ref[:, at] = (q * jnp.exp(cm + mid) * inherit).astype(BF)


def join_kernel(near_ref, far_ref, out_ref):
    near, far = near_ref[...].astype(F32), far_ref[...].astype(F32)
    decay = near[:, 128:129]
    out_ref[:, :128] = (near[:, :128] + decay * far[:, :128]).astype(BF)
    out_ref[:, 128:] = (near[:, 128:] * far[:, 128:]).astype(BF)


def reach(near_ref, far_ref, whole_ref, k):
    decay = jnp.where(whole_ref[0] == 1, near_ref[k, 128:].astype(F32)[:1], 1.0)
    return near_ref[k, :128].astype(F32) + decay * far_ref[k, :128].astype(F32)


def mixed_kernel(
    heads, whole, out_ref, qs_ref, g_ref, gain_ref, near_ref, far_ref, mixed_ref, on_ref, enter_ref
):
    for k, at in each(heads):
        enter = reach(near_ref, far_ref, whole, k)
        enter_ref[k] = enter
        mixed = out_ref[:, at] + dot_last(qs_ref[:, at], enter.astype(BF))
        mixed_ref[:, at] = mixed
        r = lax.rsqrt(jnp.mean(mixed * mixed, axis=-1, keepdims=True) + EPS)
        on_ref[:, at] = (mixed * r * gain_ref[...] * silu(g_ref[:, at])).astype(BF)


def norm_back_kernel(
    heads, don_ref, g_ref, mixed_ref, qs_ref, gain_ref, pack_ref, dmix_ref, dg_ref, dpack_ref, dgain_ref
):
    @pl.when(pl.program_id(0) == 0)
    def _():
        dgain_ref[...] = jnp.zeros_like(dgain_ref)

    gain = gain_ref[...]
    for k, at in each(heads):
        don, gz, mixed = don_ref[:, at], g_ref[:, at], mixed_ref[:, at]
        sg = sigmoid(gz)
        s = gz * sg
        r = lax.rsqrt(jnp.mean(mixed * mixed, axis=-1, keepdims=True) + EPS)
        n = mixed * r
        w = don * gain * s
        dmix = r * (w - n * jnp.mean(w * n, axis=-1, keepdims=True))
        dmix_ref[:, at] = dmix
        dg_ref[:, at] = (don * gain * n * (sg * (1.0 + gz * (1.0 - sg)))).astype(BF)
        dpack_ref[k, :128] = dot_first(dmix.astype(BF), qs_ref[:, at]).astype(BF)
        dpack_ref[k, 128:] = pack_ref[k, 128:]
        dgain_ref[...] += jnp.sum(don * s * n, axis=0, keepdims=True)


def back_kernel(
    count, heads, starts, whole, f_ref, v_ref, q_ref, b_ref, dg_ref, dmix_ref, enter_ref, near_ref,
    far_ref, dz_ref, db_ref,
):
    @pl.when(pl.program_id(0) == 0)
    def _():
        db_ref[...] = jnp.zeros_like(db_ref)

    size = f_ref.shape[0]
    same, inherit, same_last, keep = marks(starts, size, count)
    middle = about_middle(size)
    rows, cols = positions(size)
    allowed = (cols <= rows) & same
    after = ((cols >= rows) & same).astype(BF)
    mine = heads * 128
    dz_ref[:, 3 * mine :] = dg_ref[...]
    for k, at in each(heads):
        bound = b_ref[:, at]
        sg, forget, key, a = gates(f_ref[:, at], bound)
        cm = split_dot(middle, a)
        last = cm[size - 1 :]
        mid = jnp.sum(a[: size // 2], axis=0, keepdims=True)
        qz = q_ref[:, at]
        sq = sigmoid(qz)
        up, down = jnp.exp(cm), jnp.exp(-cm)
        v = v_ref[:, at].astype(BF)
        scores, qd, kd = scores_of(qz * sq * up, key * down)
        scores = jnp.where(allowed, scores, 0.0).astype(BF)
        dmix, dmix_low = halves_of(dmix_ref[:, at])
        dscores = jnp.where(allowed, dot_last(dmix, v) + dot_last(dmix_low, v), 0.0).astype(BF)
        enter = enter_ref[k]
        leave = reach(near_ref, far_ref, whole, k)
        leave_low = (leave * jnp.exp(last)).astype(BF)
        enter_low = (enter * jnp.exp(mid)).astype(BF)
        dqd = mm(dscores, kd) + inherit * mm(dmix, enter_low)
        dkd_tail = same_last * mm(v, leave_low)
        dkd = dot_first(dscores, qd) + dkd_tail
        dv = dot_first(scores, dmix) + same_last * dot_last(kd, leave_low)
        qd, kd = qd.astype(F32), kd.astype(F32)
        dlog = dqd * qd - dkd * kd
        rest = jnp.sum(dkd_tail * kd, axis=0, keepdims=True) + keep * jnp.exp(mid + last) * jnp.sum(
            leave * enter, axis=0, keepdims=True
        )
        da = split_dot(after, dlog) + same_last * rest
        dforget = da / forget - dkd * down
        dq = dqd * up * (sq * (1.0 + qz * (1.0 - sq)))
        df = dforget * (1.0 - bound) * sg * (1.0 - sg)
        for n, value in enumerate((df, dv, dq)):
            dz_ref[:, n * mine + 128 * k : n * mine + 128 * (k + 1)] = value.astype(BF)
        db_ref[:, at] += jnp.sum(dforget * (1.0 - sg), axis=0, keepdims=True)


def heads_kernel(heads, order, blocks_ref, *outs):
    for g in range(4):
        here = order[g]
        for n, out_ref in enumerate(outs):
            for k in range(heads):
                to = ((g & 1) * heads + k) * 2 + (g >> 1)
                at = n * heads + k
                out_ref[:, 128 * to : 128 * (to + 1)] = blocks_ref[
                    here, :, 128 * at : 128 * (at + 1)
                ].astype(F32)


def hidden_kernel(chunk, seqs, order, blocks_ref, *outs):
    for g in range(4):
        here = order[g]
        for n, out_ref in enumerate(outs):
            part = blocks_ref[here, :, n * seqs * chunk : (n + 1) * seqs * chunk].astype(F32)
            for j in range(seqs):
                to = (4 * j + g) * chunk
                out_ref[:, to : to + chunk] = part[:, j * chunk : (j + 1) * chunk]


def across(size, width, base=0):
    return pl.BlockSpec((size, width), lambda s, *_: (s, base))


def states(rows, heads):
    return pl.BlockSpec((heads, rows, 128), lambda s, *_: (s, 0, 0))


def fixed(width):
    return pl.BlockSpec((1, width), lambda s, *_: (0, 0))


def call(kernel, grid, scalars, in_specs, out_specs, out_shape, args, flops=1e9, vmem=48):
    params = pltpu.CompilerParams(vmem_limit_bytes=vmem * 1024 * 1024)
    return pl.pallas_call(
        kernel,
        grid_spec=pltpu.PrefetchScalarGridSpec(
            num_scalar_prefetch=len(scalars), grid=grid, in_specs=in_specs, out_specs=out_specs
        ),
        out_shape=out_shape,
        compiler_params=params,
        cost_estimate=pl.CostEstimate(flops=int(flops / 100), bytes_accessed=1 << 16, transcendentals=0),
    )(*scalars, *args)


def columns_kernel(left_ref, right_ref, out_ref):
    out_ref[...] = mm(left_ref[...], right_ref[...])


def columns(left, right, first, count):
    rows, depth = left.shape
    return call(
        columns_kernel, (count,), (),
        [
            pl.BlockSpec((rows, depth), lambda n: (0, 0)),
            pl.BlockSpec((depth, 256), lambda n: (0, n + first)),
        ],
        pl.BlockSpec((rows, 256), lambda n: (0, n)),
        jax.ShapeDtypeStruct((rows, 256 * count), F32), (left, right), 2e9 * count,
    )


def rows_kernel(left_ref, right_ref, beside_ref, gain_ref, out_ref, sum_ref):
    out = dot_last(left_ref[...], right_ref[...])
    out_ref[...] = out.astype(BF)
    sum_ref[...] = jnp.sum(out * beside_ref[...].astype(F32), axis=0, keepdims=True) / gain_ref[...]


def against_rows(left, right, beside, gain):
    rows, depth = left.shape
    wide = right.shape[0]
    block = pl.BlockSpec((rows, 256), lambda n: (0, n))
    line = pl.BlockSpec((1, 256), lambda n: (0, n))
    return call(
        rows_kernel, (wide // 256,), (),
        [
            pl.BlockSpec((rows, depth), lambda n: (0, 0)),
            pl.BlockSpec((256, depth), lambda n: (n, 0)),
            block,
            line,
        ],
        [block, line],
        [jax.ShapeDtypeStruct((rows, wide), BF), jax.ShapeDtypeStruct((1, wide), F32)],
        (left, right, beside, gain), 8e9,
    )


def join(near, far):
    pairs = near.shape[0]
    block = pl.BlockSpec((pairs // 2,) + near.shape[1:], lambda s: (s, 0, 0))
    return call(join_kernel, (2,), (), [block, block], block, jax.ShapeDtypeStruct(near.shape, BF), (near, far))


def pick_kernel(heads, place, *refs):
    *mats, last, out = refs
    k = pl.program_id(0)
    half, wide = last.shape[0], out.shape[1] - 4 * heads * 128
    for n, mat in enumerate(mats):
        out[:, pl.ds(pl.multiple_of((n * heads + k) * 128, 128), 128)] = mat[...]

    @pl.when(k == 0)
    def _():
        for n in range(4):
            out[half * n : half * (n + 1), 4 * heads * 128 :] = last[:, wide * n : wide * (n + 1)]


def picked(mats, last, heads):
    dp = lax.axis_index("dp")
    place = jnp.stack([(dp & 1) * 2 * heads + (dp >> 1), dp]).astype(jnp.int32)
    rows, width = mats[0].shape
    column = pl.BlockSpec((rows, 128), lambda k, place: (0, place[0] + 2 * k))
    return call(
        functools.partial(pick_kernel, heads), (heads,), (place,),
        [column] * 4 + [pl.BlockSpec((rows // 4, width), lambda k, place: (place[1], 0))],
        pl.BlockSpec((rows, width + width // 4), lambda k, place: (0, 0)),
        jax.ShapeDtypeStruct((rows, width + width // 4), BF), (*mats, last), vmem=62,
    )


def equal_halves(tokens):
    return lax.axis_size("seq") * tokens == 2 * MIN_LEN and MIN_LEN == 4 * tokens


def reached(pack, forward, tokens, beside):
    count = lax.axis_size("seq")
    place = lax.axis_index("seq")
    if equal_halves(tokens):
        first = [s for s in range(0, count, 4)]
        order = (0, 1, 2, 3) if forward else (3, 2, 1, 0)

        def hop(value, moves):
            return lax.ppermute(
                value, "seq", [(f + order[a], f + order[b]) for f in first for a, b in moves]
            )

        near = hop(pack, ((0, 1), (2, 3)))
        pair = join(pack, near)
        third = later(hop(pair, ((1, 3),)), beside(pair))
        second = hop(third, ((3, 2),))
        far = jnp.where((place & 3) == order[3], third, second)
        there = (place & 1) == (order[1] & 1)
        return near, far, there.astype(jnp.int32)[None]
    every = lax.all_gather(pack, "seq")
    shape = (pack.shape[0], 128, pack.shape[2])

    def one(k, total):
        at = k if forward else count - 1 - k
        there = lax.dynamic_index_in_dim(every, at, 0, False).astype(F32)
        new = there[:, :128] + there[:, 128:129] * total
        return jnp.where((at < place) if forward else (at > place), new, total)

    total = lax.fori_loop(0, count, one, jnp.zeros(shape, F32))
    total = jnp.concatenate([total, jnp.zeros_like(total[:, :16])], axis=1).astype(BF)
    total = later(total, beside(total))
    return total, jnp.zeros_like(total), jnp.ones((1,), jnp.int32)


def shards(
    block_input,
    lengths,
    norm_gain,
    w_q,
    w_f,
    w_i,
    w_g,
    lower_bound,
    group_gain,
    w_o,
    ffn_norm_gain,
    w_gate,
    w_up,
    w_down,
    out_grad,
):
    tokens, width = block_input.shape
    head_dim = group_gain.shape[0]
    heads = width // head_dim // 4
    mine = heads * head_dim
    seqs = lax.axis_size("seq")
    dp = lax.axis_index("dp")
    low_bit, high_bit = dp & 1, dp >> 1

    def of_heads(value, axis):
        shape = value.shape
        cut = value.reshape(shape[:axis] + (2, heads, 2, head_dim) + shape[axis + 1 :])
        cut = lax.dynamic_index_in_dim(cut, high_bit, axis + 2, False)
        cut = lax.dynamic_index_in_dim(cut, low_bit, axis, False)
        return cut.reshape(shape[:axis] + (mine,) + shape[axis + 1 :])

    def to_heads(blocks, axis):
        a, b, c, d = absolute(blocks)
        shape = a.shape
        cut = [v.reshape(shape[:axis] + (heads, head_dim) + shape[axis + 1 :]) for v in (a, b, c, d)]
        pair = [jnp.stack([cut[k], cut[k + 2]], axis=axis + 1) for k in range(2)]
        full = jnp.stack(pair, axis=axis)
        return full.reshape(shape[:axis] + (4 * mine,) + shape[axis + 1 :])

    chunk = w_down.shape[0] // 4
    ff = chunk * seqs

    def of_hidden(value):
        cut = value.reshape(value.shape[0], seqs, 4, chunk)
        return lax.dynamic_index_in_dim(cut, dp, 2, False).reshape(value.shape[0], ff)

    def to_hidden(blocks):
        cut = [v.reshape(v.shape[0], seqs, 1, chunk) for v in absolute(blocks)]
        return jnp.concatenate(cut, axis=2).reshape(blocks[0].shape[0], 4 * ff)

    def gather_seq(value):
        return lax.all_gather(value, "seq", axis=0, tiled=True)

    def scatter_seq(value):
        return lax.psum_scatter(value.astype(BF), "seq", scatter_dimension=0, tiled=True)

    def blocks_dp(value):
        rows = value.shape[0]
        full = gather_dp(value)
        return [full[k * rows : (k + 1) * rows] for k in range(4)]

    natural = w_o.shape[0] == 2 * head_dim
    if natural:
        both = gather_seq(picked((w_f, w_i, w_q, w_g), w_o, heads))
        halves = both[:, width:].reshape(seqs, 4, head_dim // 2, mine)
        halves = halves.transpose(0, 2, 1, 3).reshape(-1, width)
    else:
        both = gather_seq(jnp.concatenate([of_heads(w, 1) for w in (w_f, w_i, w_q, w_g)], axis=1))

    x = block_input.astype(F32)
    r1 = lax.rsqrt(jnp.mean(x * x, axis=-1, keepdims=True) + EPS)
    h = (x * r1 * norm_gain).astype(BF)

    starts = jnp.cumsum(lengths[0]) - lengths[0] - lax.axis_index("seq") * tokens
    count = lengths.shape[1]
    if equal_halves(tokens):
        starts = jnp.broadcast_to(starts[None], (4, count))
    else:
        starts = jnp.stack([starts] + [swap(starts, k) for k in (1, 2, 3)])
        h = later(h, starts)
    h_all = gather_dp(h)
    og_all = gather_dp(later(out_grad, h_all))
    blocks = 2 * mine // 256
    z_fv = columns(h_all, later(both, og_all), 0, blocks)
    w_gate, w_up = later((w_gate, w_up), h_all)
    wgu = gather_seq(jnp.concatenate([of_hidden(w_gate), of_hidden(w_up)], axis=1))
    bound = of_heads(lower_bound, 0)[None]
    gain = group_gain[None]

    grid = (4,)
    pairs = heads * 4
    rows = 4 * tokens
    wide = jax.ShapeDtypeStruct((rows, mine), F32)
    thin = jax.ShapeDtypeStruct((rows, mine), BF)
    packed = jax.ShapeDtypeStruct((pairs, 144, 128), BF)
    one = across(tokens, mine)
    fl, vl = ql, gl = across(tokens, mine, 0), across(tokens, mine, 1)
    pack_spec, state_spec = states(144, heads), states(128, heads)

    pack = call(
        functools.partial(end_kernel, count, heads), grid, (starts,),
        [fl, vl, fixed(mine)], pack_spec, packed, (z_fv, z_fv, bound), 2e9,
    )
    def within(pair):
        if natural:
            own = lax.dynamic_slice_in_dim(halves, low_bit * (mine // 2), mine // 2, 0)
            give = lax.dynamic_slice_in_dim(halves, (1 - low_bit) * (mine // 2), mine // 2, 0)
            give = later(give, pair)
            wo = pair_halves(own, swap(give, 1), low_bit, heads)
        else:
            wo = of_heads(gather_seq(w_o), 0)
            give = wo
        z_qg = columns(h_all, later(both, give), blocks, blocks)
        intra, qs = call(
            functools.partial(intra_kernel, count, heads), grid, (starts,),
            [fl, vl, ql, fixed(mine)], [one, one], [wide, thin],
            (z_fv, z_fv, z_qg, bound), 3e9,
        )
        kept.extend((wo, z_qg, intra, qs))
        return intra

    kept = []
    near, far, whole = reached(pack, True, tokens, within)
    wo, z_qg, intra, qs = kept
    w_down = later(w_down, z_qg)
    wd = gather_seq(lax.dynamic_slice_in_dim(w_down, dp * chunk, chunk, 0))
    mixed, on, enter = call(
        functools.partial(mixed_kernel, heads), grid, (whole,),
        [one, one, gl, fixed(128), pack_spec, pack_spec],
        [one, one, state_spec],
        [wide, thin, jax.ShapeDtypeStruct((pairs, 128, 128), F32)],
        (intra, qs, z_qg, gain, near, far),
    )

    branch = scatter_dp(mm(on, wo, BF))
    y = x + branch
    r2 = lax.rsqrt(jnp.mean(y * y, axis=-1, keepdims=True) + EPS)
    h2_all = gather_dp((y * r2 * ffn_norm_gain).astype(BF))

    gu = mm(h2_all, wgu)
    gate, upper = gu[:, :ff], gu[:, ff:]
    hidden = (silu(gate) * upper).astype(BF)
    down_part = dot_first(hidden, og_all, BF)
    down_rows = scatter_seq(down_part)
    d_hidden = dot_last(og_all, later(wd, down_part))
    d_gate = (d_hidden * upper * silu_grad(gate)).astype(BF)
    d_upper = (d_hidden * silu(gate)).astype(BF)
    d_gu = jnp.concatenate([d_gate, d_upper], axis=1)
    h2_part = dot_last(d_gu, wgu, BF)
    gu_part = dot_first(h2_all, later(d_gu, h2_part), BF)
    gu_rows = scatter_seq(gu_part)
    d_h2 = later(scatter_dp(h2_part), gu_part)

    og = out_grad.astype(F32)
    d_ffn_gain = jnp.sum(d_h2 * y * r2, axis=0)
    u2 = d_h2 * ffn_norm_gain
    d_y = og + r2 * u2 - y * (r2 * r2 * r2) * jnp.mean(u2 * y, axis=-1, keepdims=True)
    d_y_low, down_rows = lax.optimization_barrier((d_y.astype(BF), down_rows))
    out_part = mm(later(hidden, d_y_low), wd, BF)
    d_branch, out_part = lax.optimization_barrier((gather_dp(d_y_low), out_part))

    o_part = dot_first(on, d_branch, BF)
    d_on = dot_last(later(d_branch, o_part), wo)
    d_mixed, d_gz, d_pack, d_gain = call(
        functools.partial(norm_back_kernel, heads), grid, (),
        [one, gl, one, one, fixed(128), pack_spec],
        [one, one, pack_spec, fixed(128)],
        [wide, thin, packed, jax.ShapeDtypeStruct((1, 128), F32)],
        (d_on, z_qg, mixed, qs, gain, pack), 1e13,
    )
    def moves(pair):
        if natural:
            cut = o_part.reshape(heads, 2, head_dim // 2, width)
            own = lax.dynamic_index_in_dim(cut, low_bit, 1, False).reshape(mine // 2, width)
            give = lax.dynamic_index_in_dim(cut, 1 - low_bit, 1, False).reshape(mine // 2, width)
            got = later(swap(give, 1), pair)
            o_full = jnp.where(
                low_bit == 0,
                jnp.concatenate([own, got], axis=0),
                jnp.concatenate([got, own], axis=0),
            )
        else:
            none = jnp.zeros_like(o_part)
            o_full = got = to_heads([o_part, none, none, none], 0)
        onward, at_hand = scatter_begin(later(out_part, got))
        sent.extend((o_full, onward, at_hand))
        return onward

    sent = []
    near, far, whole = reached(d_pack, False, tokens, moves)
    o_full, onward, at_hand = sent
    o_rows = scatter_seq(o_full)
    result = (y + scatter_end(onward, at_hand)).astype(BF)

    near, far = later((near, far), o_full, result)
    dz, d_bound = call(
        functools.partial(back_kernel, count, heads), grid, (starts, whole),
        [fl, vl, ql, fixed(mine), one, one, state_spec, pack_spec, pack_spec],
        [across(tokens, 4 * mine), fixed(mine)],
        [jax.ShapeDtypeStruct((rows, 4 * mine), BF), jax.ShapeDtypeStruct((1, mine), F32)],
        (z_fv, z_fv, z_qg, bound, d_gz, d_mixed, enter, near, far), 8e9,
    )

    gu_parts = gather_begin(later(gu_rows, result))
    dz = later(dz, result, gu_parts)
    fv_part = dot_first(h_all, dz[:, : 2 * mine], BF)
    fv_rows = scatter_seq(later(fv_part, o_rows))
    h_part, d_norm_gain = against_rows(later(dz, fv_part), both, h_all, norm_gain[None])
    down_parts = gather_begin(later(down_rows, fv_part))
    h_part, down_parts = lax.optimization_barrier((h_part, down_parts))
    onward, at_hand = scatter_begin(h_part)

    zero = jnp.zeros((mine,), F32)
    d_bound = to_heads([d_bound[0], zero, zero, zero], 0)
    small = jnp.concatenate([d_norm_gain[0], d_ffn_gain, d_bound, d_gain[0]])
    extra = jnp.pad(small, (0, 32 * mine - small.shape[0])).astype(BF).reshape(1, 16, 2 * mine)
    qg_part = dot_first(h_all, later(dz, h_part)[:, 2 * mine :], BF)
    qg_part = jnp.concatenate(
        [qg_part.reshape(seqs, -1, 2 * mine), jnp.broadcast_to(extra, (seqs,) + extra.shape[1:])], axis=1
    )
    z_rows = scatter_seq(qg_part.reshape(-1, 2 * mine))

    gu_parts, down_parts, o_rows = later((gu_parts, down_parts, o_rows), onward)
    gu_parts, down_parts = gather_end(*gu_parts), gather_end(*down_parts)
    d_h = scatter_end(onward, at_hand)
    if natural:
        o_rows = later(o_rows, d_h)
        o_all = (o_rows, swap(o_rows, 1), swap(o_rows, 2), swap(o_rows, 3))
        grad_o = jnp.concatenate(absolute(o_all), axis=0).astype(F32)
    else:
        grad_o = lax.psum(o_rows.astype(F32), "dp")
    fv_parts = gather_parts(later(fv_rows, down_parts))
    qg_parts = gather_parts(later(z_rows, fv_parts[1:3], d_h))

    order = jnp.arange(4, dtype=jnp.int32) ^ dp.astype(jnp.int32)

    def whole_rows(parts, kernel, columns, flat, part=None):
        part, total = part or parts[0].shape[0], 4 * columns
        count = parts[0].shape[1] // columns
        blocks = jnp.concatenate(parts, axis=0).reshape(4, -1, count * columns)
        if not flat:
            cut = [blocks[k] for k in range(4)]
            return [
                to_hidden([v[:, k * columns : (k + 1) * columns] for v in cut]).astype(F32)
                for k in range(count)
            ]
        tall = min(64, part)
        out = jax.ShapeDtypeStruct((part, total), F32)
        return call(
            kernel, (part // tall,), (order,),
            [pl.BlockSpec((4, tall, count * columns), lambda s, *_: (0, s, 0))],
            [pl.BlockSpec((tall, total), lambda s, *_: (s, 0))] * count, [out] * count, (blocks,),
        )

    down_all = down_parts[:3] + (jnp.concatenate(down_parts[3:], axis=0),)
    grad_down = jnp.concatenate(absolute(down_all), axis=0).astype(F32)
    join_hidden = functools.partial(hidden_kernel, chunk, seqs)
    grad_gate, grad_up = whole_rows(gu_parts, join_hidden, ff, chunk % 16 == 0)
    join_heads = functools.partial(heads_kernel, heads)
    grad_f, grad_i = whole_rows(fv_parts, join_heads, mine, True)
    grad_q, grad_g = whole_rows(qg_parts, join_heads, mine, True, fv_rows.shape[0])
    small = jnp.concatenate(qg_parts, axis=0).reshape(4, -1, 2 * mine)[:, fv_rows.shape[0] :]
    small = jnp.sum(small.astype(F32), axis=0).reshape(-1)

    u1 = d_h * norm_gain
    d_x = d_y + r1 * u1 - x * (r1 * r1 * r1) * jnp.mean(u1 * x, axis=-1, keepdims=True)

    return (
        result,
        d_x.astype(BF),
        small[:width],
        grad_q,
        grad_f,
        grad_i,
        grad_g,
        small[2 * width : 3 * width],
        small[3 * width : 3 * width + head_dim],
        grad_o,
        small[width : 2 * width],
        grad_gate,
        grad_up,
        grad_down,
    )


def solution(mesh):
    both = P(("dp", "seq"), None)
    rows = P("seq", None)
    return jax.shard_map(
        shards,
        mesh=mesh,
        in_specs=(
            both, P("dp", None), P(), rows, rows, rows, rows, P(), P(), rows, P(), rows, rows, rows, both,
        ),
        out_specs=(
            both, both, P(), rows, rows, rows, rows, P(), P(), rows, P(), rows, rows, rows,
        ),
        check_vma=False,
    )
```

```python
import functools

import jax
import jax.numpy as jnp
from jax import lax
from jax.experimental import pallas as pl
from jax.experimental.pallas import tpu as pltpu
from jax.sharding import PartitionSpec as P

EPS = 1e-06
MIN_LEN = 1024
BF = jnp.bfloat16
F32 = jnp.float32


def sigmoid(value):
    return jax.nn.sigmoid(value)


def silu(value):
    return value * sigmoid(value)


def silu_grad(value):
    s = sigmoid(value)
    return s * (1.0 + value * (1.0 - s))


def mm(left, right, kind=F32):
    return jnp.dot(left, right, preferred_element_type=F32).astype(kind)


def dot_first(left, right, kind=F32):
    return lax.dot_general(
        left, right, (((0,), (0,)), ((), ())), preferred_element_type=F32
    ).astype(kind)


def dot_last(left, right, kind=F32):
    return lax.dot_general(
        left, right, (((1,), (1,)), ((), ())), preferred_element_type=F32
    ).astype(kind)


def swap(value, bits):
    count = lax.axis_size("dp")
    return lax.ppermute(value, "dp", [(s, s ^ bits) for s in range(count)])


def gather_begin(own):
    return own, swap(own, 1), swap(own, 2)


def gather_end(own, one, two):
    half = own.shape[0] // 2
    top, bottom = swap(one[:half], 2), swap(two[half:], 1)
    return own, one, two, top, bottom


def gather_parts(own):
    return gather_end(*gather_begin(own))


def gather_dp(own):
    return jnp.concatenate(gather_parts(own), axis=0)


def scatter_begin(parts):
    rows = parts.shape[0] // 4
    half = rows // 2
    p0, p1, p2, p3 = (parts[k * rows : (k + 1) * rows] for k in range(4))
    top, bottom = swap(p3[:half], 1), swap(p3[half:], 2)
    one_a, two_b = swap(p1[:half], 1), swap(p2[half:], 2)
    two_a = (p2[:half].astype(F32) + top.astype(F32)).astype(BF)
    one_b = (p1[half:].astype(F32) + bottom.astype(F32)).astype(BF)
    return (two_a, one_b), (p0, one_a, two_b)


def scatter_end(onward, at_hand):
    p0, one_a, two_b = at_hand
    two_a, one_b = swap(onward[0], 2), swap(onward[1], 1)
    one = jnp.concatenate([one_a, one_b], axis=0).astype(F32)
    two = jnp.concatenate([two_a, two_b], axis=0).astype(F32)
    return p0.astype(F32) + one + two


def scatter_dp(parts):
    return scatter_end(*scatter_begin(parts))


def later(value, *needed):
    return lax.optimization_barrier((value, needed))[0]


def pair_halves(own, other, place, heads):
    width = own.shape[1]
    own, other = (v.reshape(heads, 1, -1, width) for v in (own, other))
    both = jnp.where(
        place == 0,
        jnp.concatenate([own, other], axis=1),
        jnp.concatenate([other, own], axis=1),
    )
    return both.reshape(-1, width)


def absolute(blocks):
    place = lax.axis_index("dp")
    odd, high = (place & 1) == 1, (place & 2) == 2
    a, b, c, d = blocks
    a, b = jnp.where(odd, b, a), jnp.where(odd, a, b)
    c, d = jnp.where(odd, d, c), jnp.where(odd, c, d)
    return (
        jnp.where(high, c, a),
        jnp.where(high, d, b),
        jnp.where(high, a, c),
        jnp.where(high, b, d),
    )


def marks(starts_ref, size, count):
    slot = pl.program_id(0)
    col = lax.broadcasted_iota(jnp.int32, (size, 1), 0)
    row = lax.broadcasted_iota(jnp.int32, (1, size), 1)
    sid_c = jnp.zeros((size, 1), jnp.int32)
    sid_r = jnp.zeros((1, size), jnp.int32)
    sid_last = jnp.int32(0)
    begun = jnp.zeros((size, 1), jnp.int32)
    ended = jnp.int32(0)
    for j in range(count):
        at = starts_ref[slot, j]
        sid_c += (col >= at).astype(jnp.int32)
        sid_r += (row >= at).astype(jnp.int32)
        sid_last += (size - 1 >= at).astype(jnp.int32)
        begun += ((col >= at) & (at >= 0)).astype(jnp.int32)
        ended += ((size - 1 >= at) & (at >= 0)).astype(jnp.int32)
    inherit = (begun == 0).astype(F32)
    same_last = (sid_c == sid_last).astype(F32)
    keep = (ended == 0).astype(F32)
    return sid_c == sid_r, inherit, same_last, keep


def split_dot(left, value):
    high = value.astype(BF)
    low = (value - high.astype(F32)).astype(BF)
    return mm(left, high) + mm(left, low)


def halves_of(value):
    high = value.astype(BF)
    return high, (value - high.astype(F32)).astype(BF)


def scores_of(qd, kd):
    (qh, ql), (kh, kl) = halves_of(qd), halves_of(kd)
    return dot_last(qh, kh) + (dot_last(qh, kl) + dot_last(ql, kh)), qh, kh


def gates(f, bound):
    sg = sigmoid(f)
    forget = bound + (1.0 - bound) * sg
    return sg, forget, (1.0 - bound) * (1.0 - sg), jnp.log(forget)


def positions(size):
    rows = lax.broadcasted_iota(jnp.int32, (size, size), 0)
    cols = lax.broadcasted_iota(jnp.int32, (size, size), 1)
    return rows, cols


def about_middle(size):
    rows, cols = positions(size)
    return (cols <= rows).astype(BF) - (cols < size // 2).astype(BF)


def each(heads):
    return [(k, slice(128 * k, 128 * (k + 1))) for k in range(heads)]


def end_kernel(count, heads, starts, f_ref, v_ref, b_ref, pack_ref):
    size = f_ref.shape[0]
    _, _, same_last, keep = marks(starts, size, count)
    middle = about_middle(size)
    for k, at in each(heads):
        _, _, key, a = gates(f_ref[:, at], b_ref[:, at])
        cm = split_dot(middle, a)
        total = jnp.sum(a, axis=0, keepdims=True)
        tail = (key * jnp.exp(cm[size - 1 :] - cm) * same_last).astype(BF)
        pack_ref[k, :128] = dot_first(v_ref[:, at].astype(BF), tail).astype(BF)
        pack_ref[k, 128:] = jnp.broadcast_to(jnp.exp(total) * keep, (16, 128)).astype(BF)


def intra_kernel(count, heads, starts, f_ref, v_ref, q_ref, b_ref, out_ref, qs_ref):
    size = f_ref.shape[0]
    same, inherit, _, _ = marks(starts, size, count)
    middle = about_middle(size)
    rows, cols = positions(size)
    allowed = (cols <= rows) & same
    for _, at in each(heads):
        _, _, key, a = gates(f_ref[:, at], b_ref[:, at])
        cm = split_dot(middle, a)
        mid = jnp.sum(a[: size // 2], axis=0, keepdims=True)
        q = silu(q_ref[:, at])
        scores = jnp.where(allowed, scores_of(q * jnp.exp(cm), key * jnp.exp(-cm))[0], 0.0)
        out_ref[:, at] = mm(scores.astype(BF), v_ref[:, at].astype(BF))
        qs_ref[:, at] = (q * jnp.exp(cm + mid) * inherit).astype(BF)


def join_kernel(near_ref, far_ref, out_ref):
    near, far = near_ref[...].astype(F32), far_ref[...].astype(F32)
    decay = near[:, 128:129]
    out_ref[:, :128] = (near[:, :128] + decay * far[:, :128]).astype(BF)
    out_ref[:, 128:] = (near[:, 128:] * far[:, 128:]).astype(BF)


def reach(near_ref, far_ref, whole_ref, k):
    decay = jnp.where(whole_ref[0] == 1, near_ref[k, 128:].astype(F32)[:1], 1.0)
    return near_ref[k, :128].astype(F32) + decay * far_ref[k, :128].astype(F32)


def mixed_kernel(
    heads, whole, out_ref, qs_ref, g_ref, gain_ref, near_ref, far_ref, mixed_ref, on_ref, enter_ref
):
    for k, at in each(heads):
        enter = reach(near_ref, far_ref, whole, k)
        enter_ref[k] = enter
        mixed = out_ref[:, at] + dot_last(qs_ref[:, at], enter.astype(BF))
        mixed_ref[:, at] = mixed
        r = lax.rsqrt(jnp.mean(mixed * mixed, axis=-1, keepdims=True) + EPS)
        on_ref[:, at] = (mixed * r * gain_ref[...] * silu(g_ref[:, at])).astype(BF)


def norm_back_kernel(
    heads, don_ref, g_ref, mixed_ref, qs_ref, gain_ref, pack_ref, dmix_ref, dg_ref, dpack_ref, dgain_ref
):
    @pl.when(pl.program_id(0) == 0)
    def _():
        dgain_ref[...] = jnp.zeros_like(dgain_ref)

    gain = gain_ref[...]
    for k, at in each(heads):
        don, gz, mixed = don_ref[:, at], g_ref[:, at], mixed_ref[:, at]
        sg = sigmoid(gz)
        s = gz * sg
        r = lax.rsqrt(jnp.mean(mixed * mixed, axis=-1, keepdims=True) + EPS)
        n = mixed * r
        w = don * gain * s
        dmix = r * (w - n * jnp.mean(w * n, axis=-1, keepdims=True))
        dmix_ref[:, at] = dmix
        dg_ref[:, at] = (don * gain * n * (sg * (1.0 + gz * (1.0 - sg)))).astype(BF)
        dpack_ref[k, :128] = dot_first(dmix.astype(BF), qs_ref[:, at]).astype(BF)
        dpack_ref[k, 128:] = pack_ref[k, 128:]
        dgain_ref[...] += jnp.sum(don * s * n, axis=0, keepdims=True)


def back_kernel(
    count, heads, starts, whole, f_ref, v_ref, q_ref, b_ref, dg_ref, dmix_ref, enter_ref, near_ref,
    far_ref, dz_ref, db_ref,
):
    @pl.when(pl.program_id(0) == 0)
    def _():
        db_ref[...] = jnp.zeros_like(db_ref)

    size = f_ref.shape[0]
    same, inherit, same_last, keep = marks(starts, size, count)
    middle = about_middle(size)
    rows, cols = positions(size)
    allowed = (cols <= rows) & same
    after = ((cols >= rows) & same).astype(BF)
    mine = heads * 128
    dz_ref[:, 3 * mine :] = dg_ref[...]
    for k, at in each(heads):
        bound = b_ref[:, at]
        sg, forget, key, a = gates(f_ref[:, at], bound)
        cm = split_dot(middle, a)
        last = cm[size - 1 :]
        mid = jnp.sum(a[: size // 2], axis=0, keepdims=True)
        qz = q_ref[:, at]
        sq = sigmoid(qz)
        up, down = jnp.exp(cm), jnp.exp(-cm)
        v = v_ref[:, at].astype(BF)
        scores, qd, kd = scores_of(qz * sq * up, key * down)
        scores = jnp.where(allowed, scores, 0.0).astype(BF)
        dmix, dmix_low = halves_of(dmix_ref[:, at])
        dscores = jnp.where(allowed, dot_last(dmix, v) + dot_last(dmix_low, v), 0.0).astype(BF)
        enter = enter_ref[k]
        leave = reach(near_ref, far_ref, whole, k)
        leave_low = (leave * jnp.exp(last)).astype(BF)
        enter_low = (enter * jnp.exp(mid)).astype(BF)
        dqd = mm(dscores, kd) + inherit * mm(dmix, enter_low)
        dkd_tail = same_last * mm(v, leave_low)
        dkd = dot_first(dscores, qd) + dkd_tail
        dv = dot_first(scores, dmix) + same_last * dot_last(kd, leave_low)
        qd, kd = qd.astype(F32), kd.astype(F32)
        dlog = dqd * qd - dkd * kd
        rest = jnp.sum(dkd_tail * kd, axis=0, keepdims=True) + keep * jnp.exp(mid + last) * jnp.sum(
            leave * enter, axis=0, keepdims=True
        )
        da = split_dot(after, dlog) + same_last * rest
        dforget = da / forget - dkd * down
        dq = dqd * up * (sq * (1.0 + qz * (1.0 - sq)))
        df = dforget * (1.0 - bound) * sg * (1.0 - sg)
        for n, value in enumerate((df, dv, dq)):
            dz_ref[:, n * mine + 128 * k : n * mine + 128 * (k + 1)] = value.astype(BF)
        db_ref[:, at] += jnp.sum(dforget * (1.0 - sg), axis=0, keepdims=True)


def heads_kernel(heads, order, blocks_ref, *outs):
    for g in range(4):
        here = order[g]
        for n, out_ref in enumerate(outs):
            for k in range(heads):
                to = ((g & 1) * heads + k) * 2 + (g >> 1)
                at = n * heads + k
                out_ref[:, 128 * to : 128 * (to + 1)] = blocks_ref[
                    here, :, 128 * at : 128 * (at + 1)
                ].astype(F32)


def hidden_kernel(chunk, seqs, order, blocks_ref, *outs):
    for g in range(4):
        here = order[g]
        for n, out_ref in enumerate(outs):
            part = blocks_ref[here, :, n * seqs * chunk : (n + 1) * seqs * chunk].astype(F32)
            for j in range(seqs):
                to = (4 * j + g) * chunk
                out_ref[:, to : to + chunk] = part[:, j * chunk : (j + 1) * chunk]


def across(size, width, base=0):
    return pl.BlockSpec((size, width), lambda s, *_: (s, base))


def states(rows, heads):
    return pl.BlockSpec((heads, rows, 128), lambda s, *_: (s, 0, 0))


def fixed(width):
    return pl.BlockSpec((1, width), lambda s, *_: (0, 0))


def call(kernel, grid, scalars, in_specs, out_specs, out_shape, args, flops=1e9, vmem=48):
    params = pltpu.CompilerParams(vmem_limit_bytes=vmem * 1024 * 1024)
    return pl.pallas_call(
        kernel,
        grid_spec=pltpu.PrefetchScalarGridSpec(
            num_scalar_prefetch=len(scalars), grid=grid, in_specs=in_specs, out_specs=out_specs
        ),
        out_shape=out_shape,
        compiler_params=params,
        cost_estimate=pl.CostEstimate(flops=int(flops / 100), bytes_accessed=1 << 16, transcendentals=0),
    )(*scalars, *args)


def columns_kernel(left_ref, right_ref, out_ref):
    out_ref[...] = mm(left_ref[...], right_ref[...])


def columns(left, right, first, count):
    rows, depth = left.shape
    return call(
        columns_kernel, (count,), (),
        [
            pl.BlockSpec((rows, depth), lambda n: (0, 0)),
            pl.BlockSpec((depth, 256), lambda n: (0, n + first)),
        ],
        pl.BlockSpec((rows, 256), lambda n: (0, n)),
        jax.ShapeDtypeStruct((rows, 256 * count), F32), (left, right), 2e9 * count,
    )


def rows_kernel(left_ref, right_ref, beside_ref, gain_ref, out_ref, sum_ref):
    out = dot_last(left_ref[...], right_ref[...])
    out_ref[...] = out.astype(BF)
    sum_ref[...] = jnp.sum(out * beside_ref[...].astype(F32), axis=0, keepdims=True) / gain_ref[...]


def against_rows(left, right, beside, gain):
    rows, depth = left.shape
    wide = right.shape[0]
    block = pl.BlockSpec((rows, 256), lambda n: (0, n))
    line = pl.BlockSpec((1, 256), lambda n: (0, n))
    return call(
        rows_kernel, (wide // 256,), (),
        [
            pl.BlockSpec((rows, depth), lambda n: (0, 0)),
            pl.BlockSpec((256, depth), lambda n: (n, 0)),
            block,
            line,
        ],
        [block, line],
        [jax.ShapeDtypeStruct((rows, wide), BF), jax.ShapeDtypeStruct((1, wide), F32)],
        (left, right, beside, gain), 8e9,
    )


def join(near, far):
    pairs = near.shape[0]
    block = pl.BlockSpec((pairs // 2,) + near.shape[1:], lambda s: (s, 0, 0))
    return call(join_kernel, (2,), (), [block, block], block, jax.ShapeDtypeStruct(near.shape, BF), (near, far))


def pick_kernel(heads, place, *refs):
    *mats, last, out = refs
    k = pl.program_id(0)
    half, wide = last.shape[0], out.shape[1] - 4 * heads * 128
    for n, mat in enumerate(mats):
        out[:, pl.ds(pl.multiple_of((n * heads + k) * 128, 128), 128)] = mat[...]

    @pl.when(k == 0)
    def _():
        for n in range(4):
            out[half * n : half * (n + 1), 4 * heads * 128 :] = last[:, wide * n : wide * (n + 1)]


def picked(mats, last, heads):
    dp = lax.axis_index("dp")
    place = jnp.stack([(dp & 1) * 2 * heads + (dp >> 1), dp]).astype(jnp.int32)
    rows, width = mats[0].shape
    column = pl.BlockSpec((rows, 128), lambda k, place: (0, place[0] + 2 * k))
    return call(
        functools.partial(pick_kernel, heads), (heads,), (place,),
        [column] * 4 + [pl.BlockSpec((rows // 4, width), lambda k, place: (place[1], 0))],
        pl.BlockSpec((rows, width + width // 4), lambda k, place: (0, 0)),
        jax.ShapeDtypeStruct((rows, width + width // 4), BF), (*mats, last), vmem=62,
    )


def equal_halves(tokens):
    return lax.axis_size("seq") * tokens == 2 * MIN_LEN and MIN_LEN == 4 * tokens


def reached(pack, forward, tokens, beside):
    count = lax.axis_size("seq")
    place = lax.axis_index("seq")
    if equal_halves(tokens):
        first = [s for s in range(0, count, 4)]
        order = (0, 1, 2, 3) if forward else (3, 2, 1, 0)

        def hop(value, moves):
            return lax.ppermute(
                value, "seq", [(f + order[a], f + order[b]) for f in first for a, b in moves]
            )

        near = hop(pack, ((0, 1), (2, 3)))
        pair = join(pack, near)
        third = later(hop(pair, ((1, 3),)), beside(pair))
        second = hop(third, ((3, 2),))
        far = jnp.where((place & 3) == order[3], third, second)
        there = (place & 1) == (order[1] & 1)
        return near, far, there.astype(jnp.int32)[None]
    every = lax.all_gather(pack, "seq")
    shape = (pack.shape[0], 128, pack.shape[2])

    def one(k, total):
        at = k if forward else count - 1 - k
        there = lax.dynamic_index_in_dim(every, at, 0, False).astype(F32)
        new = there[:, :128] + there[:, 128:129] * total
        return jnp.where((at < place) if forward else (at > place), new, total)

    total = lax.fori_loop(0, count, one, jnp.zeros(shape, F32))
    total = jnp.concatenate([total, jnp.zeros_like(total[:, :16])], axis=1).astype(BF)
    total = later(total, beside(total))
    return total, jnp.zeros_like(total), jnp.ones((1,), jnp.int32)


def shards(
    block_input,
    lengths,
    norm_gain,
    w_q,
    w_f,
    w_i,
    w_g,
    lower_bound,
    group_gain,
    w_o,
    ffn_norm_gain,
    w_gate,
    w_up,
    w_down,
    out_grad,
):
    tokens, width = block_input.shape
    head_dim = group_gain.shape[0]
    heads = width // head_dim // 4
    mine = heads * head_dim
    seqs = lax.axis_size("seq")
    dp = lax.axis_index("dp")
    low_bit, high_bit = dp & 1, dp >> 1

    def of_heads(value, axis):
        shape = value.shape
        cut = value.reshape(shape[:axis] + (2, heads, 2, head_dim) + shape[axis + 1 :])
        cut = lax.dynamic_index_in_dim(cut, high_bit, axis + 2, False)
        cut = lax.dynamic_index_in_dim(cut, low_bit, axis, False)
        return cut.reshape(shape[:axis] + (mine,) + shape[axis + 1 :])

    def to_heads(blocks, axis):
        a, b, c, d = absolute(blocks)
        shape = a.shape
        cut = [v.reshape(shape[:axis] + (heads, head_dim) + shape[axis + 1 :]) for v in (a, b, c, d)]
        pair = [jnp.stack([cut[k], cut[k + 2]], axis=axis + 1) for k in range(2)]
        full = jnp.stack(pair, axis=axis)
        return full.reshape(shape[:axis] + (4 * mine,) + shape[axis + 1 :])

    chunk = w_down.shape[0] // 4
    ff = chunk * seqs

    def of_hidden(value):
        cut = value.reshape(value.shape[0], seqs, 4, chunk)
        return lax.dynamic_index_in_dim(cut, dp, 2, False).reshape(value.shape[0], ff)

    def to_hidden(blocks):
        cut = [v.reshape(v.shape[0], seqs, 1, chunk) for v in absolute(blocks)]
        return jnp.concatenate(cut, axis=2).reshape(blocks[0].shape[0], 4 * ff)

    def gather_seq(value):
        return lax.all_gather(value, "seq", axis=0, tiled=True)

    def scatter_seq(value):
        return lax.psum_scatter(value.astype(BF), "seq", scatter_dimension=0, tiled=True)

    def blocks_dp(value):
        rows = value.shape[0]
        full = gather_dp(value)
        return [full[k * rows : (k + 1) * rows] for k in range(4)]

    natural = w_o.shape[0] == 2 * head_dim
    if natural:
        both = gather_seq(picked((w_f, w_i, w_q, w_g), w_o, heads))
        halves = both[:, width:].reshape(seqs, 4, head_dim // 2, mine)
        halves = halves.transpose(0, 2, 1, 3).reshape(-1, width)
    else:
        both = gather_seq(jnp.concatenate([of_heads(w, 1) for w in (w_f, w_i, w_q, w_g)], axis=1))

    x = block_input.astype(F32)
    r1 = lax.rsqrt(jnp.mean(x * x, axis=-1, keepdims=True) + EPS)
    h = (x * r1 * norm_gain).astype(BF)

    starts = jnp.cumsum(lengths[0]) - lengths[0] - lax.axis_index("seq") * tokens
    count = lengths.shape[1]
    if equal_halves(tokens):
        starts = jnp.broadcast_to(starts[None], (4, count))
    else:
        starts = jnp.stack([starts] + [swap(starts, k) for k in (1, 2, 3)])
        h = later(h, starts)
    h_all = gather_dp(h)
    og_all = gather_dp(later(out_grad, h_all))
    blocks = 2 * mine // 256
    z_fv = columns(h_all, later(both, og_all), 0, blocks)
    w_gate, w_up = later((w_gate, w_up), h_all)
    wgu = gather_seq(jnp.concatenate([of_hidden(w_gate), of_hidden(w_up)], axis=1))
    bound = of_heads(lower_bound, 0)[None]
    gain = group_gain[None]

    grid = (4,)
    pairs = heads * 4
    rows = 4 * tokens
    wide = jax.ShapeDtypeStruct((rows, mine), F32)
    thin = jax.ShapeDtypeStruct((rows, mine), BF)
    packed = jax.ShapeDtypeStruct((pairs, 144, 128), BF)
    one = across(tokens, mine)
    fl, vl = ql, gl = across(tokens, mine, 0), across(tokens, mine, 1)
    pack_spec, state_spec = states(144, heads), states(128, heads)

    pack = call(
        functools.partial(end_kernel, count, heads), grid, (starts,),
        [fl, vl, fixed(mine)], pack_spec, packed, (z_fv, z_fv, bound), 2e9,
    )
    def within(pair):
        if natural:
            own = lax.dynamic_slice_in_dim(halves, low_bit * (mine // 2), mine // 2, 0)
            give = lax.dynamic_slice_in_dim(halves, (1 - low_bit) * (mine // 2), mine // 2, 0)
            give = later(give, pair)
            wo = pair_halves(own, swap(give, 1), low_bit, heads)
        else:
            wo = of_heads(gather_seq(w_o), 0)
            give = wo
        z_qg = columns(h_all, later(both, give), blocks, blocks)
        intra, qs = call(
            functools.partial(intra_kernel, count, heads), grid, (starts,),
            [fl, vl, ql, fixed(mine)], [one, one], [wide, thin],
            (z_fv, z_fv, z_qg, bound), 3e9,
        )
        kept.extend((wo, z_qg, intra, qs))
        return intra

    kept = []
    near, far, whole = reached(pack, True, tokens, within)
    wo, z_qg, intra, qs = kept
    w_down = later(w_down, z_qg)
    wd = gather_seq(lax.dynamic_slice_in_dim(w_down, dp * chunk, chunk, 0))
    mixed, on, enter = call(
        functools.partial(mixed_kernel, heads), grid, (whole,),
        [one, one, gl, fixed(128), pack_spec, pack_spec],
        [one, one, state_spec],
        [wide, thin, jax.ShapeDtypeStruct((pairs, 128, 128), F32)],
        (intra, qs, z_qg, gain, near, far),
    )

    branch = scatter_dp(mm(on, wo, BF))
    y = x + branch
    r2 = lax.rsqrt(jnp.mean(y * y, axis=-1, keepdims=True) + EPS)
    h2_all = gather_dp((y * r2 * ffn_norm_gain).astype(BF))

    gu = mm(h2_all, wgu)
    gate, upper = gu[:, :ff], gu[:, ff:]
    hidden = (silu(gate) * upper).astype(BF)
    down_part = dot_first(hidden, og_all, BF)
    down_rows = scatter_seq(down_part)
    d_hidden = dot_last(og_all, later(wd, down_part))
    d_gate = (d_hidden * upper * silu_grad(gate)).astype(BF)
    d_upper = (d_hidden * silu(gate)).astype(BF)
    d_gu = jnp.concatenate([d_gate, d_upper], axis=1)
    h2_part = dot_last(d_gu, wgu, BF)
    gu_part = dot_first(h2_all, later(d_gu, h2_part), BF)
    gu_rows = scatter_seq(gu_part)
    d_h2 = later(scatter_dp(h2_part), gu_part)

    og = out_grad.astype(F32)
    d_ffn_gain = jnp.sum(d_h2 * y * r2, axis=0)
    u2 = d_h2 * ffn_norm_gain
    d_y = og + r2 * u2 - y * (r2 * r2 * r2) * jnp.mean(u2 * y, axis=-1, keepdims=True)
    d_y_low, down_rows = lax.optimization_barrier((d_y.astype(BF), down_rows))
    out_part = mm(later(hidden, d_y_low), wd, BF)
    d_branch, out_part = lax.optimization_barrier((gather_dp(d_y_low), out_part))

    o_part = dot_first(on, d_branch, BF)
    d_on = dot_last(later(d_branch, o_part), wo)
    d_mixed, d_gz, d_pack, d_gain = call(
        functools.partial(norm_back_kernel, heads), grid, (),
        [one, gl, one, one, fixed(128), pack_spec],
        [one, one, pack_spec, fixed(128)],
        [wide, thin, packed, jax.ShapeDtypeStruct((1, 128), F32)],
        (d_on, z_qg, mixed, qs, gain, pack), 1e13,
    )
    def moves(pair):
        if natural:
            cut = o_part.reshape(heads, 2, head_dim // 2, width)
            own = lax.dynamic_index_in_dim(cut, low_bit, 1, False).reshape(mine // 2, width)
            give = lax.dynamic_index_in_dim(cut, 1 - low_bit, 1, False).reshape(mine // 2, width)
            got = later(swap(give, 1), pair)
            o_full = jnp.where(
                low_bit == 0,
                jnp.concatenate([own, got], axis=0),
                jnp.concatenate([got, own], axis=0),
            )
        else:
            none = jnp.zeros_like(o_part)
            o_full = got = to_heads([o_part, none, none, none], 0)
        onward, at_hand = scatter_begin(later(out_part, got))
        sent.extend((o_full, onward, at_hand))
        return onward

    sent = []
    near, far, whole = reached(d_pack, False, tokens, moves)
    o_full, onward, at_hand = sent
    o_rows = scatter_seq(o_full)
    result = (y + scatter_end(onward, at_hand)).astype(BF)

    near, far = later((near, far), o_full, result)
    dz, d_bound = call(
        functools.partial(back_kernel, count, heads), grid, (starts, whole),
        [fl, vl, ql, fixed(mine), one, one, state_spec, pack_spec, pack_spec],
        [across(tokens, 4 * mine), fixed(mine)],
        [jax.ShapeDtypeStruct((rows, 4 * mine), BF), jax.ShapeDtypeStruct((1, mine), F32)],
        (z_fv, z_fv, z_qg, bound, d_gz, d_mixed, enter, near, far), 8e9,
    )

    gu_parts = gather_begin(later(gu_rows, result))
    dz = later(dz, result, gu_parts)
    fvq_part = dot_first(h_all, dz[:, : 3 * mine], BF)
    fvq_rows = scatter_seq(later(fvq_part, o_rows))
    h_part, d_norm_gain = against_rows(later(dz, fvq_part), both, h_all, norm_gain[None])
    down_parts = gather_begin(later(down_rows, fvq_part))
    h_part, down_parts = lax.optimization_barrier((h_part, down_parts))
    onward, at_hand = scatter_begin(h_part)

    zero = jnp.zeros((mine,), F32)
    d_bound = to_heads([d_bound[0], zero, zero, zero], 0)
    small = jnp.concatenate([d_norm_gain[0], d_ffn_gain, d_bound, d_gain[0]])
    extra = jnp.pad(small, (0, 16 * mine - small.shape[0])).astype(BF).reshape(1, 16, mine)
    g_part = dot_first(h_all, later(dz, h_part)[:, 3 * mine :], BF)
    g_part = jnp.concatenate(
        [g_part.reshape(seqs, -1, mine), jnp.broadcast_to(extra, (seqs,) + extra.shape[1:])], axis=1
    )
    z_rows = scatter_seq(g_part.reshape(-1, mine))

    gu_parts, down_parts, o_rows = later((gu_parts, down_parts, o_rows), onward)
    gu_parts, down_parts = gather_end(*gu_parts), gather_end(*down_parts)
    d_h = scatter_end(onward, at_hand)
    if natural:
        o_rows = later(o_rows, d_h)
        o_all = (o_rows, swap(o_rows, 1), swap(o_rows, 2), swap(o_rows, 3))
        grad_o = jnp.concatenate(absolute(o_all), axis=0).astype(F32)
    else:
        grad_o = lax.psum(o_rows.astype(F32), "dp")
    fvq_parts = gather_parts(later(fvq_rows, down_parts))
    g_parts = gather_parts(later(z_rows, fvq_parts[1:3], d_h))

    order = jnp.arange(4, dtype=jnp.int32) ^ dp.astype(jnp.int32)

    def whole_rows(parts, kernel, columns, flat, part=None):
        part, total = part or parts[0].shape[0], 4 * columns
        count = parts[0].shape[1] // columns
        blocks = jnp.concatenate(parts, axis=0).reshape(4, -1, count * columns)
        if not flat:
            cut = [blocks[k] for k in range(4)]
            return [
                to_hidden([v[:, k * columns : (k + 1) * columns] for v in cut]).astype(F32)
                for k in range(count)
            ]
        tall = min(64, part)
        out = jax.ShapeDtypeStruct((part, total), F32)
        return call(
            kernel, (part // tall,), (order,),
            [pl.BlockSpec((4, tall, count * columns), lambda s, *_: (0, s, 0))],
            [pl.BlockSpec((tall, total), lambda s, *_: (s, 0))] * count, [out] * count, (blocks,),
        )

    down_all = down_parts[:3] + (jnp.concatenate(down_parts[3:], axis=0),)
    grad_down = jnp.concatenate(absolute(down_all), axis=0).astype(F32)
    join_hidden = functools.partial(hidden_kernel, chunk, seqs)
    grad_gate, grad_up = whole_rows(gu_parts, join_hidden, ff, chunk % 16 == 0)
    join_heads = functools.partial(heads_kernel, heads)
    grad_f, grad_i, grad_q = whole_rows(fvq_parts, join_heads, mine, True)
    [grad_g] = whole_rows(g_parts, join_heads, mine, True, fvq_rows.shape[0])
    small = jnp.concatenate(g_parts, axis=0).reshape(4, -1, mine)[:, fvq_rows.shape[0] :]
    small = jnp.sum(small.astype(F32), axis=0).reshape(-1)

    u1 = d_h * norm_gain
    d_x = d_y + r1 * u1 - x * (r1 * r1 * r1) * jnp.mean(u1 * x, axis=-1, keepdims=True)

    return (
        result,
        d_x.astype(BF),
        small[:width],
        grad_q,
        grad_f,
        grad_i,
        grad_g,
        small[2 * width : 3 * width],
        small[3 * width : 3 * width + head_dim],
        grad_o,
        small[width : 2 * width],
        grad_gate,
        grad_up,
        grad_down,
    )


def solution(mesh):
    both = P(("dp", "seq"), None)
    rows = P("seq", None)
    return jax.shard_map(
        shards,
        mesh=mesh,
        in_specs=(
            both, P("dp", None), P(), rows, rows, rows, rows, P(), P(), rows, P(), rows, rows, rows, both,
        ),
        out_specs=(
            both, both, P(), rows, rows, rows, rows, P(), P(), rows, P(), rows, rows, rows,
        ),
        check_vma=False,
    )
```
